256 devices in a mesh: view: 4 (over z_hi), block: 64 (over y, x, z_lo, core).
Axes of the slice: x: 4, y: 4, z: 8 (z_hi: 4, z_lo: 2; z = z_hi * 2 + z_lo), core: 2. Of those that a mesh axis runs over, the one named last changes fastest.
Arguments:
- view_tiles: bfloat16 [4, 5120, 24, 1024], P('view', 'block'), may hold values from 0.25 to 4
- route_block: int32 [4, 5120], P('view', 'block'), may hold values from 0 to 63, as said below
- route_column: int32 [4, 5120], P('view', 'block'), may hold values from 0 to 31, as said below
- psf_taps: float32 [4, 3, 31], P('view'), may hold values from 0.002 to 1.5
- start_estimate: float32 [24, 2048, 1024], P(None, 'block'), may hold values from 0.5 to 2
Outputs:
- estimate: float32 [24, 2048, 1024], P(None, 'block')
The draws below stay inside these ranges and needn't reach their ends.
Inputs may be any that keep to these rules, and one draw needn't show every extreme that they name: `route_block`: for each view, every column of every block receives at least one tile column; at most 2 tile columns held by one device go to one block, and in every draw some block receives exactly 2 from every device. `route_column`: column within the receiving block.
All inputs are finite; a program needn't handle non-finite values.
Results may differ from the reference program's by a relative error of at most 0.00071.
Values may be sent and summed in bfloat16 or wider, within the bound.
No kernel may reach another device: no remote copies, remote signals or barrier semaphores. Data moves between devices by JAX's collectives and lax.ppermute only.
A program may use at most 128 MiB of HBM per device.

```python
import math
import jax
import jax.numpy as jnp
from jax import lax

BX = 32
NY = 1024
NZ = 24
TAPS = 31
ITERS = 2
HALF = 15
VIEWS = 4
NX = 2048
CAP = 2
PIECE_DEV = 80
PIECES = 5120
N_BLOCK = 64


def draw_routes(key):
    spare = N_BLOCK * CAP - BX

    def one_view(view_key):
        key_order, key_split, key_spread, key_shuffle = jax.random.split(view_key, 4)
        order = jax.random.permutation(key_order, N_BLOCK)
        splits = jax.random.randint(key_split, (N_BLOCK // 2,), 0, spare + 1)
        splits = splits.at[0].set(0)
        extra = jnp.zeros((N_BLOCK,), jnp.int32)
        extra = extra.at[order[0::2]].set(spare - splits)
        extra = extra.at[order[1::2]].set(splits)
        counts = BX + extra
        ends = jnp.cumsum(counts)
        starts = ends - counts
        places = jnp.arange(N_BLOCK * PIECE_DEV, dtype=jnp.int32)
        target = jnp.sum((places[:, None] >= ends[None, :]).astype(jnp.int32), axis=1)
        within = places - starts[target]
        spread = jax.random.randint(key_spread, (N_BLOCK * PIECE_DEV,), 0, BX)
        column = jnp.where(within < BX, within, spread)
        source = places % N_BLOCK
        position = places // N_BLOCK
        shuffles = jax.vmap(lambda inner: jax.random.permutation(inner, PIECE_DEV))(jax.random.split(key_shuffle, N_BLOCK))
        placed = shuffles[source, position]
        blocks_out = jnp.zeros((N_BLOCK, PIECE_DEV), jnp.int32).at[source, placed].set(target)
        columns_out = jnp.zeros((N_BLOCK, PIECE_DEV), jnp.int32).at[source, placed].set(column)
        return (blocks_out.reshape(N_BLOCK * PIECE_DEV), columns_out.reshape(N_BLOCK * PIECE_DEV))
    return jax.vmap(one_view)(jax.random.split(key, VIEWS))


def draw_route_block(key, part):
    shared = draw_routes(key)
    return shared[0]


def draw_route_column(key, part):
    shared = draw_routes(key)
    return shared[1]


def draw_view_tiles(key, part):
    key = jax.random.fold_in(key, 3)
    key_base, key_level = jax.random.split(key)
    step_rows = max(1, NY // 64)
    count_levels = (NY + step_rows - 1) // step_rows
    base = jnp.exp(jax.random.uniform(key_base, (VIEWS, PIECES, NZ, NY), jnp.float32, -1.0, 1.0))
    levels = jax.random.uniform(key_level, (VIEWS, count_levels), jnp.float32, -0.6, 0.6)
    level_of = jnp.exp(levels)[:, jnp.arange(NY, dtype=jnp.int32) // step_rows]
    values = base * level_of[:, None, None, :]
    return jnp.clip(values, 0.25, 4.0).astype(jnp.bfloat16)


def draw_psf_taps(key, part):
    key = jax.random.fold_in(key, 4)
    key_order, key_offset, key_rough = jax.random.split(key, 3)
    orders = jax.vmap(lambda inner: jax.random.permutation(inner, VIEWS))(jax.random.split(key_order, 3))
    offsets = jax.random.uniform(key_offset, (VIEWS, 3), jnp.float32, 0.0, 1.0)
    ranks = jnp.transpose(orders).astype(jnp.float32)
    widths = 1.5 * (2.0 * HALF / 1.5) ** ((ranks + offsets) / VIEWS)
    places = jnp.arange(TAPS, dtype=jnp.float32) - HALF
    envelope = jnp.exp(-0.5 * (places[None, None, :] / widths[:, :, None]) ** 2)
    rough = jnp.exp(jax.random.uniform(key_rough, (VIEWS, 3, TAPS), jnp.float32, -0.35, 0.35))
    return envelope * rough + 0.002


def block_scale(own_key, extent, shards, low, high):
    gain, own = 1.0, jax.random.fold_in(own_key, 6)
    for axis_at, parts in shards:
        steps = jnp.exp(jax.random.uniform(jax.random.fold_in(own, axis_at), (parts,), jnp.float32, low / len(shards), high / len(shards)))
        gain = gain * jnp.repeat(steps, extent[axis_at] // parts).reshape([-1 if axis == axis_at else 1 for axis in range(len(extent))])
    return gain


def setup_inputs(seed: int = 0) -> dict:
    keys = jax.random.split(jax.random.key(seed), 6)
    return {
        "view_tiles": draw_view_tiles(jax.random.fold_in(keys[5], 71), 0),
        "route_block": draw_route_block(jax.random.fold_in(keys[5], 71), 0),
        "route_column": draw_route_column(jax.random.fold_in(keys[5], 71), 0),
        "psf_taps": draw_psf_taps(jax.random.fold_in(keys[5], 71), 0),
        "start_estimate": jnp.clip(jnp.exp(math.log(2.0) - 1.3862944 * jax.random.uniform(keys[4], (NZ, NX, NY), jnp.float32) ** block_scale(keys[4], (NZ, NX, NY), ((1, 64),), -0.2, 0.2)), 0.5, 2.0),
    }


def to_half(values):
    return lax.optimization_barrier(values.astype(jnp.bfloat16)).astype(jnp.float32)


def smear(field, axis_index, weights, mirrored):
    count_taps = weights.shape[0]
    margin = (count_taps - 1) // 2
    widths = [(0, 0), (0, 0), (0, 0)]
    widths[axis_index] = (margin, margin)
    padded = jnp.pad(to_half(field), widths)
    length = field.shape[axis_index]
    result = jnp.zeros(field.shape, jnp.float32)
    for tap_index in range(count_taps):
        if mirrored:
            weight = weights[count_taps - 1 - tap_index]
        else:
            weight = weights[tap_index]
        result = result + weight * lax.slice_in_dim(padded, tap_index, tap_index + length, axis=axis_index)
    return result


def blur_all(field, kernel, mirrored):
    field = smear(field, 1, kernel[1], mirrored)
    field = smear(field, 2, kernel[2], mirrored)
    return smear(field, 0, kernel[0], mirrored)


def reference(view_tiles, route_block, route_column, psf_taps, start_estimate):
    kernel = to_half(psf_taps / jnp.sum(psf_taps, axis=2, keepdims=True))
    measured = []
    for view_index in range(VIEWS):
        landing = (route_block[view_index] * BX + route_column[view_index]).astype(jnp.int32)
        summed = jax.ops.segment_sum(view_tiles[view_index].astype(jnp.float32), landing, num_segments=NX)
        covered = jax.ops.segment_sum(jnp.ones(landing.shape, jnp.float32), landing, num_segments=NX)
        measured.append(jnp.transpose(summed / covered[:, None, None], (1, 0, 2)))
    estimate = start_estimate
    for iteration in range(ITERS):
        correction = jnp.zeros(start_estimate.shape, jnp.float32)
        for view_index in range(VIEWS):
            quotient = measured[view_index] / blur_all(estimate, kernel[view_index], False)
            correction = correction + blur_all(quotient, kernel[view_index], True)
        estimate = estimate * correction / VIEWS
    return estimate
```

```python
import functools

import jax
import jax.numpy as jnp
import numpy as np
from jax import lax
from jax.experimental import pallas as pl
from jax.experimental.pallas import tpu as pltpu
from jax.sharding import PartitionSpec as P

ITERS = 2
TAPS = 31
HALF = 15
VIEWS = 4
NZ = 24
BX = 32
MARGIN = 16
EX = BX + 2 * MARGIN
YQ = 256
YE = 384
TURN = 320
ROWS = BX * NZ
ZI = 8
ZG = NZ // ZI
XR = BX * ZI
EXR = EX * ZI
GX = 8
GR = GX * ZI
ZR = GX * NZ
FULL = 32700.0
STEPS = 128.0
LN2 = float(np.log(2.0))
M_MID, M_SCALE = 2.125, 32767.0 / 1.875
E_SCALE = 32767.0 / 2.0
VMEM = 56 * 1024 * 1024

f32, bf16, i32, i16 = jnp.float32, jnp.bfloat16, jnp.int32, jnp.int16


def params():
    return pltpu.CompilerParams(vmem_limit_bytes=VMEM)


def cost(flops, moved):
    return pl.CostEstimate(flops=int(flops), bytes_accessed=int(moved), transcendentals=0)


def dot(a, b):
    return jnp.dot(a, b, preferred_element_type=f32)


def halves(x):
    hi = x.astype(bf16)
    return hi, (x - hi.astype(f32)).astype(bf16)


def to_code(x):
    return jnp.floor(x + 0.5).astype(i32).astype(i16)


def from_code(c):
    return c.astype(i32).astype(f32)


def scale_steps(top):
    return jnp.ceil(jnp.log(jnp.maximum(top, 1e-30)) * (STEPS / LN2))


def lane_code(value):
    k = scale_steps(jnp.max(jnp.abs(value), axis=0, keepdims=True))
    code = to_code(value * (jnp.exp(k * (-LN2 / STEPS)) * FULL))
    return code, jnp.broadcast_to(k, (16, value.shape[1])).astype(i32).astype(i16)


def lane_value(ref):
    n = ref.shape[0] - 16
    k = from_code(ref[n:])[0:1]
    return from_code(ref[:n]) * (jnp.exp(k * (LN2 / STEPS)) * (1.0 / FULL))


def send(ref, value):
    n = value.shape[0]
    ref[:n], ref[n:] = lane_code(value)


def flat(x):
    return x.reshape(x.shape[0] * x.shape[1], x.shape[2])


LOADS = 4
SLOT = NZ * 8


def pack_body(cap, blocks, columns, tiles, out, labels, count, slots, held, sent, loaded, sem):
    pieces = tiles.shape[0]
    part = pieces // LOADS
    groups = out.shape[0]

    def load(i):
        rows = pl.ds(i * part, part)
        return pltpu.make_async_copy(tiles.at[rows], held.at[rows], loaded.at[i])

    for i in range(LOADS):
        load(i).start()

    def clear(i, _):
        labels[i] = 0
        return 0

    lax.fori_loop(0, groups * cap, clear, 0)

    def zero(i, _):
        count[i] = 0
        return 0

    lax.fori_loop(0, groups, zero, 0)

    def route(p, _):
        b = blocks[p]
        rank = count[b]
        count[b] = rank + 1
        slot = b * cap + rank
        labels[slot] = columns[p] + 1
        slots[p] = slot
        return 0

    lax.fori_loop(0, pieces, route, 0)
    lane = lax.broadcasted_iota(i32, (16, 128), 1)

    def mark(b, _):
        row = jnp.zeros((16, 128), i32)
        for rank in range(cap):
            row = jnp.where(lane == rank, labels[b * cap + rank], row)
        sent[b, cap * SLOT :, :] = row.astype(f32).astype(bf16)
        return 0

    lax.fori_loop(0, groups, mark, 0)
    for i in range(LOADS):
        load(i).wait()

        def put(p, _):
            slot = slots[p]
            b = slot // cap
            at = (slot - b * cap) * SLOT
            for c in range(8):
                rows = pl.ds(pl.multiple_of(at + 16 * c, 16), 16)
                sent[b, rows, :] = held[p, :16, 128 * c : 128 * (c + 1)]
            for c in range(0, 8, 2):
                rows = pl.ds(pl.multiple_of(at + 128 + 8 * c, 16), 16)
                sent[b, rows, :] = jnp.concatenate(
                    [
                        held[p, 16:, 128 * c : 128 * (c + 1)],
                        held[p, 16:, 128 * (c + 1) : 128 * (c + 2)],
                    ],
                    axis=0,
                )
            return 0

        lax.fori_loop(i * part, (i + 1) * part, put, 0, unroll=2)
    push = pltpu.make_async_copy(sent, out, sem)
    push.start()
    push.wait()


def pack(cap, groups, blocks, columns, tiles):
    smem = pl.BlockSpec(memory_space=pltpu.SMEM)
    message = (groups, cap * SLOT + 16, 128)
    return pl.pallas_call(
        functools.partial(pack_body, cap),
        out_shape=jax.ShapeDtypeStruct(message, bf16),
        in_specs=[smem, smem, pl.BlockSpec(memory_space=pl.ANY)],
        out_specs=pl.BlockSpec(memory_space=pl.ANY),
        scratch_shapes=[
            pltpu.SMEM((groups * cap,), i32),
            pltpu.SMEM((groups,), i32),
            pltpu.SMEM((tiles.shape[0],), i32),
            pltpu.VMEM(tiles.shape, bf16),
            pltpu.VMEM(message, bf16),
            pltpu.SemaphoreType.DMA((LOADS,)),
            pltpu.SemaphoreType.DMA,
        ],
        compiler_params=params(),
        cost_estimate=cost(0, 4 * tiles.size),
    )(blocks, columns, tiles)


def unpack_body(cap, chunk, place, arrived, whole_arrived, *rest):
    outs, (acc, count, marks, table, labels, sem) = rest[:VIEWS], rest[VIEWS:]
    step = pl.program_id(0)
    layer = place[1]

    @pl.when(step == 0)
    def _():
        fetch = pltpu.make_async_copy(
            whole_arrived.at[:, pl.ds(cap * SLOT, 16), :], marks, sem.at[0]
        )
        fetch.start()
        acc[...] = jnp.zeros_like(acc)

        def zero(i, _):
            count[i] = 0
            return 0

        lax.fori_loop(0, BX, zero, 0)
        fetch.wait()
        table[...] = jnp.max(marks[...].astype(f32), axis=1).astype(i32)
        move = pltpu.make_async_copy(table, labels, sem.at[1])
        move.start()
        move.wait()

    for j in range(chunk):
        for rank in range(cap):
            label = labels[step * chunk + j, rank]

            @pl.when(label > 0)
            def _():
                col = label - 1
                rows = pl.ds(pl.multiple_of(col * ZI, ZI), ZI)
                tile = arrived[j, rank * SLOT : (rank + 1) * SLOT, :].astype(f32)
                for c in range(8):
                    lanes = slice(128 * c, 128 * (c + 1))
                    acc[0, rows, lanes] += tile[16 * c : 16 * c + 8]
                    acc[1, rows, lanes] += tile[16 * c + 8 : 16 * c + 16]
                    acc[2, rows, lanes] += tile[128 + 8 * c : 136 + 8 * c]
                count[col] += 1

    @pl.when(step == pl.num_programs(0) - 1)
    def _():
        row = lax.broadcasted_iota(i32, (2 * ZI, 128), 0)
        lane = lax.broadcasted_iota(i32, (2 * ZI, 128), 1)

        def pair(i, _):
            first = M_SCALE / jnp.maximum(count[2 * i], 1).astype(f32)
            second = M_SCALE / jnp.maximum(count[2 * i + 1], 1).astype(f32)
            inverse = jnp.where(row < ZI, first, second)
            for g in range(ZG):
                rows = pl.ds(pl.multiple_of(i * 2 * ZI, 2 * ZI), 2 * ZI)
                to = pl.ds(pl.multiple_of(g * XR + i * 2 * ZI, 2 * ZI), 2 * ZI)

                def code_at(lane_block):
                    lanes = pl.ds(pl.multiple_of(lane_block * 128, 128), 128)
                    code = acc[g, rows, lanes] * inverse - M_MID * M_SCALE
                    return jnp.clip(code, -32767.0, 32767.0)

                for r in range(VIEWS):
                    base = 2 * lax.rem(layer + r, VIEWS)
                    after = code_at(jnp.minimum(base + 2, 2 * VIEWS - 1))
                    before = code_at(jnp.maximum(base - 1, 0))
                    outs[r][to, 0:128] = to_code(code_at(base))
                    outs[r][to, 128:256] = to_code(code_at(base + 1))
                    outs[r][to, 256:384] = to_code(jnp.where(lane < 64, after, before))
            return 0

        lax.fori_loop(0, BX // 2, pair, 0)


def unpack(cap, place, arrived):
    groups = arrived.shape[0]
    chunk = min(8, groups)
    smem = pl.BlockSpec(memory_space=pltpu.SMEM)
    return pl.pallas_call(
        functools.partial(unpack_body, cap, chunk),
        grid=(groups // chunk,),
        out_shape=(jax.ShapeDtypeStruct((ROWS, YE), i16),) * VIEWS,
        in_specs=[
            smem,
            pl.BlockSpec((chunk,) + arrived.shape[1:], lambda s: (s, 0, 0)),
            pl.BlockSpec(memory_space=pl.ANY),
        ],
        out_specs=(pl.BlockSpec((ROWS, YE), lambda s: (0, 0)),) * VIEWS,
        scratch_shapes=[
            pltpu.VMEM((ZG, XR, VIEWS * YQ), f32),
            pltpu.SMEM((BX,), i32),
            pltpu.VMEM((groups, 16, 128), bf16),
            pltpu.VMEM((groups, 128), i32),
            pltpu.SMEM((groups, 128), i32),
            pltpu.SemaphoreType.DMA((2,)),
        ],
        compiler_params=params(),
        cost_estimate=cost(arrived.size, 2 * arrived.size),
    )(place, arrived, arrived)


def iota(shape, dim):
    return lax.broadcasted_iota(i32, shape, dim)


def bands_body(taps, kx, kxt, ty, tyt, bz, bzt):
    r = pl.program_id(0)

    def band(distance, axis):
        out = jnp.zeros(distance.shape, f32)
        for t in range(TAPS):
            out = jnp.where(distance == t, taps[r, axis * TAPS + t], out)
        return out

    def kept(x):
        return lax.shift_right_logical(x, 3)

    def inner(x):
        return lax.bitwise_and(x, ZI - 1)

    row, col = iota((XR, EXR), 0), iota((XR, EXR), 1)
    same = inner(row) == inner(col)
    kx[0] = jnp.where(same, band(kept(col) - kept(row) - 1, 1), 0.0).astype(bf16)
    row, col = iota((EXR, XR), 0), iota((EXR, XR), 1)
    same = inner(row) == inner(col)
    kxt[0] = jnp.where(same, band(kept(row) - kept(col) - 1, 1), 0.0).astype(bf16)

    def place(k):
        return jnp.where(k < TURN, k, k - YE)

    apart = place(iota((YE, YE), 0)) - place(iota((YE, YE), 1))
    ty[0] = band(apart + HALF, 2).astype(bf16)
    back = band(HALF - apart, 2).astype(bf16)
    tyt[0, :YE] = back
    tyt[0, YE:] = back

    def parts(x):
        group = jnp.where(x >= 2 * GR, 2, jnp.where(x >= GR, 1, 0))
        within = x - group * GR
        return group * ZI + inner(within), kept(within)

    (zr, xr), (zc, xc) = parts(iota((ZR, ZR), 0)), parts(iota((ZR, ZR), 1))
    bz[0] = jnp.where(xr == xc, band(zc - zr + HALF, 0), 0.0).astype(bf16)
    (zr, xr), col = parts(iota((ZR, 2 * ZR), 0)), iota((ZR, 2 * ZR), 1)
    zc, xc = parts(jnp.where(col >= ZR, col - ZR, col))
    bzt[0] = jnp.where(xr == xc, band(zr - zc + HALF, 0), 0.0).astype(bf16)


MATS = [(XR, EXR), (EXR, XR), (YE, YE), (2 * YE, YE), (ZR, ZR), (ZR, 2 * ZR)]


def bands(taps):
    return pl.pallas_call(
        bands_body,
        grid=(VIEWS,),
        out_shape=tuple(jax.ShapeDtypeStruct((VIEWS,) + s, bf16) for s in MATS),
        in_specs=[pl.BlockSpec(memory_space=pltpu.SMEM)],
        out_specs=tuple(pl.BlockSpec((1,) + s, lambda r: (r, 0, 0)) for s in MATS),
        compiler_params=params(),
        cost_estimate=cost(4e9, 2e7),
    )(taps)


def cell_body(place, start, own, left, right, scratch):
    layer = place[1]
    last = start.shape[2] - 128
    after = jnp.minimum((layer + 1) * YQ, last)
    before = jnp.maximum(layer * YQ - 128, 0)
    lane = iota((BX, 128), 1)
    for z in range(NZ):
        rows = pl.ds(z // ZI * XR + z % ZI, BX, stride=ZI)
        for c in range(2):
            at = pl.multiple_of(layer * YQ + c * 128, 128)
            scratch[c, rows, :] = start[z, :, pl.ds(at, 128)]
        head = start[z, :, pl.ds(pl.multiple_of(after, 128), 128)]
        tail = start[z, :, pl.ds(pl.multiple_of(before, 128), 128)]
        head = jnp.where((lane < TURN - YQ) & (layer < VIEWS - 1), head, 0.0)
        tail = jnp.where((lane >= TURN - YQ) & (layer > 0), tail, 0.0)
        scratch[2, rows, :] = head + tail
    value = jnp.concatenate([scratch[c] for c in range(3)], axis=1)
    own[...] = value.reshape(ZG, XR, YE)
    code = to_code(value * E_SCALE).reshape(ZG, XR, YE)
    left[...] = code[:, : XR // 2]
    right[...] = code[:, XR // 2 :]


def cell(place, start):
    half = jax.ShapeDtypeStruct((ZG, XR // 2, YE), i16)
    return pl.pallas_call(
        cell_body,
        out_shape=(jax.ShapeDtypeStruct((ZG, XR, YE), f32), half, half),
        in_specs=[
            pl.BlockSpec(memory_space=pltpu.SMEM),
            pl.BlockSpec(memory_space=pltpu.VMEM),
        ],
        scratch_shapes=[pltpu.VMEM((3, ROWS, 128), f32)],
        compiler_params=params(),
        cost_estimate=cost(3e6, 6e6),
    )(place, start)


def blurred(field, kx, ty, bz):
    x = jnp.concatenate([dot(kx, field[g]).astype(bf16) for g in range(ZG)], axis=0)
    y = dot(x, ty).astype(bf16)
    return [dot(bz, columns_of(y, XR, c)) for c in range(BX // GX)]


def columns_of(rows, stride, c):
    return jnp.concatenate(
        [rows[g * stride + c * GR : g * stride + (c + 1) * GR] for g in range(ZG)], axis=0
    )


def rows_from(groups):
    return jnp.concatenate(
        [part[g * GR : (g + 1) * GR] for g in range(ZG) for part in groups], axis=0
    )


def mirrored(quotient, kxt, tyt, bzt, pairs):
    parts = [halves(dot(kxt, quotient[g * XR : (g + 1) * XR])) for g in range(ZG)]
    hi = jnp.concatenate([p[0] for p in parts], axis=0)
    lo = jnp.concatenate([p[1] for p in parts], axis=0)
    for c in range(EX // GX):
        both = jnp.concatenate([columns_of(hi, EXR, c), columns_of(lo, EXR, c)], axis=0)
        z_hi, z_lo = halves(dot(bzt, both))
        for g in range(ZG):
            rows = slice(g * EXR + c * GR, g * EXR + (c + 1) * GR)
            pairs[rows, :YE] = z_hi[g * GR : (g + 1) * GR]
            pairs[rows, YE:] = z_lo[g * GR : (g + 1) * GR]
    return dot(pairs[...], tyt)


def quotient_of(layer, code, blur_now):
    lane = iota(code.shape, 1)
    inside = (lane < YQ) | ((lane < TURN) & (layer < VIEWS - 1)) | ((lane >= TURN) & (layer > 0))
    measured = jnp.where(inside, from_code(code) * (1.0 / M_SCALE) + M_MID, 0.0)
    return (measured / jnp.where(inside, blur_now, 1.0)).astype(bf16)


def widened(own, from_left, from_right):
    inverse = 1.0 / E_SCALE
    return jnp.concatenate(
        [from_code(from_left) * inverse, own, from_code(from_right) * inverse], axis=1
    )


def mat_spec(n, at=None):
    index = (lambda r: (r, 0, 0)) if at is None else (lambda *_: (at, 0, 0))
    return pl.BlockSpec((1,) + MATS[n], index)


def whole(shape):
    return pl.BlockSpec(shape, lambda *_: (0,) * len(shape))


def blur_body(own, from_left, from_right, kx, ty, bz, out, field):
    @pl.when(pl.program_id(0) == 0)
    def _():
        field[...] = widened(own[...], from_left[...], from_right[...]).astype(bf16)

    out[0] = rows_from(blurred(field, kx[0], ty[0], bz[0]))


def blur(own, from_left, from_right, mats):
    return pl.pallas_call(
        blur_body,
        grid=(VIEWS,),
        out_shape=jax.ShapeDtypeStruct((VIEWS, ROWS, YE), f32),
        in_specs=[
            whole(own.shape),
            whole(from_left.shape),
            whole(from_right.shape),
            mat_spec(0),
            mat_spec(2),
            mat_spec(4),
        ],
        out_specs=pl.BlockSpec((1, ROWS, YE), lambda r: (r, 0, 0)),
        scratch_shapes=[pltpu.VMEM((ZG, EXR, YE), bf16)],
        compiler_params=params(),
        cost_estimate=cost(7e9, 1.6e7),
    )(own, from_left, from_right, mats[0], mats[2], mats[4])


def mirror_body(first, last, place, code, blur_ref, kxt, tyt, bzt, *rest):
    rest, pairs = list(rest[:-1]), rest[-1]
    before = None if first else rest.pop(0)
    total = rest.pop(0)
    quotient = quotient_of(place[1], code[...], blur_ref[0])
    value = mirrored(quotient, kxt[0], tyt[0], bzt[0], pairs).reshape(ZG, EXR, YE)
    if not first:
        value = value + before[...]
    total[...] = value
    if last:
        left, right = rest
        send(left, flat(value[:, : EXR // 2]))
        send(right, flat(value[:, EXR // 2 :]))


def mirror(r, place, code, blur_all, mats, before):
    first, last = r == 0, r == VIEWS - 1
    columns = jax.ShapeDtypeStruct((ZG * EXR // 2 + 16, YE), i16)
    shapes = [jax.ShapeDtypeStruct((ZG, EXR, YE), f32)] + [columns, columns] * last
    operands = [place, code, blur_all, mats[1], mats[3], mats[5]] + [before] * (not first)
    return pl.pallas_call(
        functools.partial(mirror_body, first, last),
        grid=(1,),
        out_shape=tuple(shapes),
        in_specs=[
            pl.BlockSpec(memory_space=pltpu.SMEM),
            whole(code.shape),
            pl.BlockSpec((1, ROWS, YE), lambda *_: (r, 0, 0)),
            mat_spec(1, r),
            mat_spec(3, r),
            mat_spec(5, r),
        ]
        + [whole((ZG, EXR, YE))] * (not first),
        out_specs=tuple(whole(s.shape) for s in shapes),
        scratch_shapes=[pltpu.VMEM((ZG * EXR, 2 * YE), bf16)],
        compiler_params=params(),
        cost_estimate=cost(2e9, 8e6),
    )(*operands)


def second_body(place, own, e_left, e_right, total, x_left, x_right, *rest):
    codes = rest[:VIEWS]
    kx, kxt, ty, tyt, bz, bzt = rest[VIEWS : VIEWS + 6]
    estimate, center, left, right, field, acc, pairs = rest[VIEWS + 6 :]
    step = pl.program_id(0)
    edge = MARGIN * ZI
    middle = EXR // 2

    @pl.when(step == 0)
    def _():
        start = widened(own[...], e_left[...], e_right[...]) * (1.0 / VIEWS)
        for half, came in enumerate((x_left, x_right)):
            rows = slice(half * middle, (half + 1) * middle)
            now = start[:, rows] * (total[:, rows] + lane_value(came).reshape(ZG, middle, YE))
            field[:, rows] = now.astype(bf16)
            inner = now[:, edge:] if half == 0 else now[:, : middle - edge]
            estimate[:, half * edge : (half + 1) * edge] = inner[:, :, :YQ]
        acc[...] = jnp.zeros_like(acc)

    code = codes[0][...].astype(i32)
    for r in range(1, VIEWS):
        code = jnp.where(step == r, codes[r][...].astype(i32), code)
    blur_now = rows_from(blurred(field, kx[0], ty[0], bz[0]))
    quotient = quotient_of(place[1], code, blur_now)
    acc[...] += mirrored(quotient, kxt[0], tyt[0], bzt[0], pairs).reshape(ZG, EXR, YE)

    @pl.when(step == pl.num_programs(0) - 1)
    def _():
        center[...] = acc[:, edge : edge + XR, :YQ]
        send(left, flat(acc[:, :edge, :YQ]))
        send(right, flat(acc[:, edge + XR :, :YQ]))


def second(place, own, e_left, e_right, total, x_left, x_right, codes, mats):
    columns = jax.ShapeDtypeStruct((ZG * MARGIN * ZI + 16, YQ), i16)
    cell_shape = jax.ShapeDtypeStruct((ZG, XR, YQ), f32)
    shapes = (cell_shape, cell_shape, columns, columns)
    operands = (own, e_left, e_right, total, x_left, x_right) + tuple(codes)
    return pl.pallas_call(
        second_body,
        grid=(VIEWS,),
        out_shape=shapes,
        in_specs=[pl.BlockSpec(memory_space=pltpu.SMEM)]
        + [whole(a.shape) for a in operands]
        + [mat_spec(n) for n in range(6)],
        out_specs=tuple(whole(s.shape) for s in shapes),
        scratch_shapes=[
            pltpu.VMEM((ZG, EXR, YE), bf16),
            pltpu.VMEM((ZG, EXR, YE), f32),
            pltpu.VMEM((ZG * EXR, 2 * YE), bf16),
        ],
        compiler_params=params(),
        cost_estimate=cost(1.6e10, 4e7),
    )(place, *operands, *mats)


def finish_body(estimate, total, x_left, x_right, out):
    middle = XR // 2
    low = total[:, :middle] + lane_value(x_left).reshape(ZG, middle, YQ)
    high = total[:, middle:] + lane_value(x_right).reshape(ZG, middle, YQ)
    summed = jnp.concatenate([low, high], axis=1)
    send(out, flat(estimate[...] * summed * (1.0 / VIEWS)))


def finish(estimate, total, x_left, x_right):
    return pl.pallas_call(
        finish_body,
        out_shape=jax.ShapeDtypeStruct((ROWS + 16, YQ), i16),
        compiler_params=params(),
        cost_estimate=cost(5e6, 4e6),
    )(estimate, total, x_left, x_right)


def gather_body(place, *rest):
    codes, out, scratch = rest[:VIEWS], rest[VIEWS], rest[VIEWS + 1]
    layer = place[1]
    for r in range(VIEWS):
        value = lane_value(codes[r])
        at = lax.rem(layer + VIEWS - r, VIEWS) * YQ
        for c in range(2):
            scratch[r, c] = value[:, c * 128 : (c + 1) * 128]
            lanes = pl.ds(pl.multiple_of(at + c * 128, 128), 128)
            for z in range(NZ):
                rows = pl.ds(z // ZI * XR + z % ZI, BX, stride=ZI)
                out[z, :, lanes] = scratch[r, c, rows, :]


def gathered(place, codes):
    return pl.pallas_call(
        gather_body,
        out_shape=jax.ShapeDtypeStruct((NZ, BX, VIEWS * YQ), f32),
        in_specs=[pl.BlockSpec(memory_space=pltpu.SMEM)]
        + [pl.BlockSpec(memory_space=pltpu.VMEM)] * VIEWS,
        scratch_shapes=[pltpu.VMEM((VIEWS, 2, ROWS, 128), f32)],
        compiler_params=params(),
        cost_estimate=cost(3e6, 6e6),
    )(place, *codes)


def per_device(view_tiles, route_block, route_column, psf_taps, start_estimate):
    groups = lax.axis_size("block")
    cap = max(2, (2 * BX + groups - 1) // groups)
    me, layer = lax.axis_index("block"), lax.axis_index("view")
    place = jnp.stack([me, layer]).astype(i32)

    def around(x, shift):
        return lax.ppermute(x, "view", [(i, (i + shift) % VIEWS) for i in range(VIEWS)])

    def shifted(x, shift):
        pairs = [(i, i + shift) for i in range(groups) if 0 <= i + shift < groups]
        return lax.ppermute(x, "block", pairs)

    kernel = psf_taps[0] / jnp.sum(psf_taps[0], axis=1, keepdims=True)
    kernel = kernel.astype(bf16).astype(f32)
    taps = jnp.stack([kernel] + [around(kernel, r) for r in range(1, VIEWS)])

    outgoing = pack(cap, groups, route_block[0], route_column[0], view_tiles[0])
    outgoing, taps = lax.optimization_barrier((outgoing, taps))
    arrived = lax.all_to_all(outgoing, "block", split_axis=0, concat_axis=0, tiled=True)

    mats = bands(taps.reshape(VIEWS, 3 * TAPS))
    start_estimate, _ = lax.optimization_barrier((start_estimate, outgoing))
    own, to_left, to_right = cell(place, start_estimate)
    e_left, e_right = shifted(to_right, 1), shifted(to_left, -1)

    codes = unpack(cap, place, arrived)
    own, codes = lax.optimization_barrier((own, codes))
    codes = [codes[0]] + [around(codes[r], r) for r in range(1, VIEWS)]
    blur_all = blur(own, e_left, e_right, mats)
    parts = [None]
    for r in range(VIEWS):
        parts = mirror(r, place, codes[r], blur_all, mats, parts[0])
    total, left, right = parts
    x_left, x_right = shifted(right, 1), shifted(left, -1)
    estimate, center, left, right = second(
        place, own, e_left, e_right, total, x_left, x_right, codes, mats
    )
    x_left, x_right = shifted(right, 1), shifted(left, -1)
    final = finish(estimate, center, x_left, x_right)
    return gathered(place, [final] + [around(final, r) for r in range(1, VIEWS)])


def solution(mesh):
    placed = (
        P("view", "block", None, None),
        P("view", "block"),
        P("view", "block"),
        P("view", None, None),
        P(None, "block", None),
    )
    return jax.shard_map(
        per_device, mesh=mesh, in_specs=placed, out_specs=P(None, "block", None), check_vma=False
    )
```

```python
import functools

import jax
import jax.numpy as jnp
import numpy as np
from jax import lax
from jax.experimental import pallas as pl
from jax.experimental.pallas import tpu as pltpu
from jax.sharding import PartitionSpec as P

ITERS = 2
TAPS = 31
HALF = 15
VIEWS = 4
NZ = 24
BX = 32
MARGIN = 16
EX = BX + 2 * MARGIN
YQ = 256
YE = 384
TURN = 320
ROWS = BX * NZ
ZI = 8
ZG = NZ // ZI
XR = BX * ZI
EXR = EX * ZI
GX = 8
GR = GX * ZI
ZR = GX * NZ
FULL = 32700.0
STEPS = 128.0
LN2 = float(np.log(2.0))
M_MID, M_SCALE = 2.125, 32767.0 / 1.875
E_SCALE = 32767.0 / 2.0
VMEM = 28 * 1024 * 1024

f32, bf16, i32, i16 = jnp.float32, jnp.bfloat16, jnp.int32, jnp.int16


def params(limit=VMEM):
    return pltpu.CompilerParams(vmem_limit_bytes=limit)


KEPT = pl.BlockSpec(memory_space=pltpu.VMEM)


def kept(operands):
    return [pltpu.with_memory_space_constraint(x, pltpu.VMEM) for x in operands]


def cost(flops, moved):
    return pl.CostEstimate(flops=int(flops), bytes_accessed=int(moved), transcendentals=0)


def dot(a, b):
    return jnp.dot(a, b, preferred_element_type=f32)


def to_code(x):
    return jnp.floor(x + 0.5).astype(i32).astype(i16)


def from_code(c):
    return c.astype(i32).astype(f32)


def scale_steps(top):
    return jnp.ceil(jnp.log(jnp.maximum(top, 1e-30)) * (STEPS / LN2))


def lane_code(value):
    k = scale_steps(jnp.max(jnp.abs(value), axis=0, keepdims=True))
    code = to_code(value * (jnp.exp(k * (-LN2 / STEPS)) * FULL))
    return code, jnp.broadcast_to(k, (16, value.shape[1])).astype(i32).astype(i16)


def lane_value(ref):
    n = ref.shape[0] - 16
    k = from_code(ref[n:])[0:1]
    return from_code(ref[:n]) * (jnp.exp(k * (LN2 / STEPS)) * (1.0 / FULL))


def send(ref, value):
    n = value.shape[0]
    ref[:n], ref[n:] = lane_code(value)


def flat(x):
    return x.reshape(x.shape[0] * x.shape[1], x.shape[2])


LOADS = 4
SLOT = NZ * 8


def pack_body(cap, blocks, columns, tiles, out, labels, count, slots, held, sent, loaded, pushed):
    pieces = tiles.shape[0]
    part = pieces // LOADS
    groups = out.shape[0]

    def load(i):
        rows = pl.ds(i * part, part)
        return pltpu.make_async_copy(tiles.at[rows], held.at[rows], loaded.at[i])

    for i in range(LOADS):
        load(i).start()

    def clear(i, _):
        labels[i] = 0
        return 0

    lax.fori_loop(0, groups * cap, clear, 0)

    def zero(i, _):
        count[i] = 0
        return 0

    lax.fori_loop(0, groups, zero, 0)

    def route(p, _):
        b = blocks[p]
        rank = count[b]
        count[b] = rank + 1
        slot = b * cap + rank
        labels[slot] = columns[p] + 1
        slots[p] = slot
        return 0

    lax.fori_loop(0, pieces, route, 0)
    lane = lax.broadcasted_iota(i32, (16, 128), 1)

    def mark(b, _):
        row = jnp.zeros((16, 128), i32)
        for rank in range(cap):
            row = jnp.where(lane == rank, labels[b * cap + rank], row)
        sent[b, cap * SLOT :, :] = row.astype(f32).astype(bf16)
        return 0

    lax.fori_loop(0, groups, mark, 0)
    def push(b, at, rows, sem):
        part = pl.ds(pl.multiple_of(at, 16), rows)
        return pltpu.make_async_copy(sent.at[b, part, :], out.at[b, part, :], sem)

    def tags():
        rows = pl.ds(cap * SLOT, 16)
        return pltpu.make_async_copy(sent.at[:, rows, :], out.at[:, rows, :], pushed.at[1])

    tags().start()
    for i in range(LOADS):
        load(i).wait()

        def put(p, _):
            slot = slots[p]
            b = slot // cap
            at = (slot - b * cap) * SLOT
            for c in range(8):
                rows = pl.ds(pl.multiple_of(at + 16 * c, 16), 16)
                sent[b, rows, :] = held[p, :16, 128 * c : 128 * (c + 1)]
            for c in range(0, 8, 2):
                rows = pl.ds(pl.multiple_of(at + 128 + 8 * c, 16), 16)
                sent[b, rows, :] = jnp.concatenate(
                    [
                        held[p, 16:, 128 * c : 128 * (c + 1)],
                        held[p, 16:, 128 * (c + 1) : 128 * (c + 2)],
                    ],
                    axis=0,
                )
            push(b, at, SLOT, pushed.at[0]).start()
            return 0

        lax.fori_loop(i * part, (i + 1) * part, put, 0, unroll=2)
    tags().wait()
    if pieces % cap == 0:
        every = pl.ds(0, pieces // cap), pl.ds(0, cap * SLOT)
        pltpu.make_async_copy(sent.at[every], out.at[every], pushed.at[0]).wait()
    else:
        lax.fori_loop(0, pieces, lambda p, _: push(0, 0, SLOT, pushed.at[0]).wait(), None)


def pack(cap, groups, blocks, columns, tiles):
    smem = pl.BlockSpec(memory_space=pltpu.SMEM)
    message = (groups, cap * SLOT + 16, 128)
    return pl.pallas_call(
        functools.partial(pack_body, cap),
        out_shape=pltpu.HBM(message, bf16),
        in_specs=[smem, smem, pl.BlockSpec(memory_space=pltpu.HBM)],
        out_specs=pl.BlockSpec(memory_space=pltpu.HBM),
        scratch_shapes=[
            pltpu.SMEM((groups * cap,), i32),
            pltpu.SMEM((groups,), i32),
            pltpu.SMEM((tiles.shape[0],), i32),
            pltpu.VMEM(tiles.shape, bf16),
            pltpu.VMEM(message, bf16),
            pltpu.SemaphoreType.DMA((LOADS,)),
            pltpu.SemaphoreType.DMA((2,)),
        ],
        compiler_params=params(2 * VMEM),
        cost_estimate=cost(0, 4 * tiles.size),
    )(blocks, columns, pltpu.with_memory_space_constraint(tiles, pltpu.HBM))


PART_VIEWS = (0, 1, 2, 2, 3)
PART_ROWS = (0, 0, 0, ROWS // 2, 0)


def unpack_body(cap, chunk, place, arrived, whole_arrived, *rest):
    outs, (acc, codes, count, marks, table, labels, sem) = rest[: VIEWS + 1], rest[VIEWS + 1 :]
    step = pl.program_id(0)
    layer = place[1]

    @pl.when(step == 0)
    def _():
        fetch = pltpu.make_async_copy(
            whole_arrived.at[:, pl.ds(cap * SLOT, 16), :], marks, sem.at[0]
        )
        fetch.start()
        acc[...] = jnp.zeros_like(acc)

        def zero(i, _):
            count[i] = 0
            return 0

        lax.fori_loop(0, BX, zero, 0)
        fetch.wait()
        ranks = table.shape[0]
        which = jnp.where(iota((ranks, 128), 0) == iota((ranks, 128), 1), 1.0, 0.0)
        lines = jnp.max(marks[...].astype(f32), axis=1)
        found = lax.dot_general(which, lines, (((1,), (1,)), ((), ())), preferred_element_type=f32)
        table[:, : lines.shape[0]] = found.astype(i32)
        move = pltpu.make_async_copy(table, labels, sem.at[1])
        move.start()
        move.wait()

    for j in range(chunk):
        for rank in range(cap):
            label = labels[rank, step * chunk + j]

            @pl.when(label > 0)
            def _():
                col = label - 1
                rows = pl.ds(pl.multiple_of(col * ZI, ZI), ZI)
                tile = arrived[j, rank * SLOT : (rank + 1) * SLOT, :].astype(f32)
                for c in range(8):
                    lanes = slice(128 * c, 128 * (c + 1))
                    acc[0, rows, lanes] += tile[16 * c : 16 * c + 8]
                    acc[1, rows, lanes] += tile[16 * c + 8 : 16 * c + 16]
                    acc[2, rows, lanes] += tile[128 + 8 * c : 136 + 8 * c]
                count[col] += 1

    @pl.when(step == pl.num_programs(0) - 1)
    def _():
        row = lax.broadcasted_iota(i32, (2 * ZI, 128), 0)
        lane = lax.broadcasted_iota(i32, (2 * ZI, 128), 1)

        def pair(i, _):
            first = M_SCALE / jnp.maximum(count[2 * i], 1).astype(f32)
            second = M_SCALE / jnp.maximum(count[2 * i + 1], 1).astype(f32)
            inverse = jnp.where(row < ZI, first, second)
            for g in range(ZG):
                rows = pl.ds(pl.multiple_of(i * 2 * ZI, 2 * ZI), 2 * ZI)
                to = pl.ds(pl.multiple_of(g * XR + i * 2 * ZI, 2 * ZI), 2 * ZI)
                blocks = [
                    acc[g, rows, 128 * c : 128 * (c + 1)] * inverse - M_MID * M_SCALE
                    for c in range(2 * VIEWS)
                ]
                for v in range(VIEWS):
                    after = blocks[min(2 * v + 2, 2 * VIEWS - 1)]
                    before = blocks[max(2 * v - 1, 0)]
                    ends = jnp.where(lane < 64, after, before)
                    code = jnp.concatenate([blocks[2 * v], blocks[2 * v + 1], ends], axis=1)
                    codes[v, to, :] = to_code(code)
            return 0

        lax.fori_loop(0, BX // 2, pair, 0, unroll=4)
        for r, at, out in zip(PART_VIEWS, PART_ROWS, outs):
            out[...] = codes[lax.rem(layer + r, VIEWS), at : at + out.shape[0], :]


def unpack(cap, place, arrived):
    groups = arrived.shape[0]
    chunk = min(32, groups)
    shapes = [(ROWS // PART_VIEWS.count(r), YE) for r in PART_VIEWS]
    smem = pl.BlockSpec(memory_space=pltpu.SMEM)
    return pl.pallas_call(
        functools.partial(unpack_body, cap, chunk),
        grid=(groups // chunk,),
        out_shape=tuple(jax.ShapeDtypeStruct(shape, i16) for shape in shapes),
        in_specs=[
            smem,
            pl.BlockSpec((chunk,) + arrived.shape[1:], lambda s: (s, 0, 0)),
            pl.BlockSpec(memory_space=pl.ANY),
        ],
        out_specs=tuple(pl.BlockSpec(shape, lambda s: (0, 0)) for shape in shapes),
        scratch_shapes=[
            pltpu.VMEM((ZG, XR, VIEWS * YQ), f32),
            pltpu.VMEM((VIEWS, ROWS, YE), i16),
            pltpu.SMEM((BX,), i32),
            pltpu.VMEM((groups, 16, 128), bf16),
            pltpu.VMEM((max(8, cap), 128), i32),
            pltpu.SMEM((max(8, cap), 128), i32),
            pltpu.SemaphoreType.DMA((2,)),
        ],
        compiler_params=params(),
        cost_estimate=cost(arrived.size, 2 * arrived.size),
    )(place, arrived, arrived)


def iota(shape, dim):
    return lax.broadcasted_iota(i32, shape, dim)


def bands_body(taps, kx, kxt, ty, tyt, bz, bzt):
    r = pl.program_id(0)

    def band(distance, axis):
        out = jnp.zeros(distance.shape, f32)
        for t in range(TAPS):
            out = jnp.where(distance == t, taps[r, axis * TAPS + t], out)
        return out

    def circulant(row, n):
        wide = jnp.broadcast_to(row[0:1], (n, row.shape[1]))
        return pltpu.roll(wide, 0, 1, stride=1, stride_axis=0).astype(bf16)

    m = iota((8, EXR), 1)
    aligned = lax.bitwise_and(m, ZI - 1) == 0
    taps_at = band(lax.shift_right_logical(m, 3) - 1, 1)
    kx[r] = circulant(jnp.where(aligned, taps_at, 0.0), XR)
    taps_at = band(lax.shift_right_logical(EXR - m, 3) - 1, 1)
    kxt[r] = circulant(jnp.where(aligned, taps_at, 0.0), EXR)[:, :XR]
    n = iota((8, YE), 1)
    apart = jnp.where(n < YE // 2, n, n - YE)
    ty[r] = circulant(band(HALF - apart, 2), YE)
    back = circulant(band(HALF + apart, 2), YE)
    tyt[r] = back

    def parts(x):
        group = jnp.where(x >= 2 * GR, 2, jnp.where(x >= GR, 1, 0))
        within = x - group * GR
        return group * ZI + lax.bitwise_and(within, ZI - 1), lax.shift_right_logical(within, 3)

    (zr, xr), (zc, xc) = parts(iota((ZR, 1), 0)), parts(iota((1, ZR), 1))
    same = xr == xc
    bz[r] = jnp.where(same, band(zc - zr + HALF, 0), 0.0).astype(bf16)
    bzt[r] = jnp.where(same, band(zr - zc + HALF, 0), 0.0).astype(bf16)


MATS = [(XR, EXR), (EXR, XR), (YE, YE), (YE, YE), (ZR, ZR), (ZR, ZR)]


def bands(taps):
    return pl.pallas_call(
        bands_body,
        grid=(VIEWS,),
        out_shape=tuple(pltpu.VMEM((VIEWS,) + s, bf16) for s in MATS),
        in_specs=[pl.BlockSpec(memory_space=pltpu.SMEM)],
        out_specs=(KEPT,) * len(MATS),
        compiler_params=params(),
        cost_estimate=cost(4e9, 2e7),
    )(taps)


def cell_body(place, start, own, left, right, scratch):
    layer = place[1]
    last = start.shape[2] - 128
    after = jnp.minimum((layer + 1) * YQ, last)
    before = jnp.maximum(layer * YQ - 128, 0)
    lane = iota((BX, 128), 1)
    for z in range(NZ):
        rows = pl.ds(z // ZI * XR + z % ZI, BX, stride=ZI)
        for c in range(2):
            at = pl.multiple_of(layer * YQ + c * 128, 128)
            scratch[c, rows, :] = start[z, :, pl.ds(at, 128)]
        head = start[z, :, pl.ds(pl.multiple_of(after, 128), 128)]
        tail = start[z, :, pl.ds(pl.multiple_of(before, 128), 128)]
        head = jnp.where((lane < TURN - YQ) & (layer < VIEWS - 1), head, 0.0)
        tail = jnp.where((lane >= TURN - YQ) & (layer > 0), tail, 0.0)
        scratch[2, rows, :] = head + tail
    value = jnp.concatenate([scratch[c] for c in range(3)], axis=1)
    own[...] = value.reshape(ZG, XR, YE)
    code = to_code(value * E_SCALE).reshape(ZG, XR, YE)
    left[...] = code[:, : XR // 2]
    right[...] = code[:, XR // 2 :]


def cell(place, start):
    half = jax.ShapeDtypeStruct((ZG, XR // 2, YE), i16)
    return pl.pallas_call(
        cell_body,
        out_shape=(pltpu.VMEM((ZG, XR, YE), f32), half, half),
        in_specs=[
            pl.BlockSpec(memory_space=pltpu.SMEM),
            pl.BlockSpec(memory_space=pltpu.VMEM),
        ],
        scratch_shapes=[pltpu.VMEM((3, ROWS, 128), f32)],
        compiler_params=params(),
        cost_estimate=cost(3e6, 6e6),
    )(place, start)


def blurred_columns(field, kx, out):
    for g in range(ZG):
        x = dot(kx[...].reshape(VIEWS * XR, EXR), field[g]).astype(bf16)
        out[:, g * XR : (g + 1) * XR, :] = x.reshape(VIEWS, XR, YE)


def blurred(x, ty, bz):
    y = dot(x, ty).astype(bf16)
    return [dot(bz, columns_of(y, XR, c)) for c in range(BX // GX)]


def columns_of(rows, stride, c):
    return jnp.concatenate(
        [rows[g * stride + c * GR : g * stride + (c + 1) * GR] for g in range(ZG)], axis=0
    )


def rows_from(groups):
    return jnp.concatenate(
        [part[g * GR : (g + 1) * GR] for g in range(ZG) for part in groups], axis=0
    )


def mirrored(quotient, kxt, tyt, bzt, out, first):
    y = dot(quotient, tyt).astype(bf16)
    x = [dot(kxt, y[g * XR : (g + 1) * XR]).astype(bf16) for g in range(ZG)]
    for c in range(EX // GX):
        rows = slice(c * GR, (c + 1) * GR)
        z = dot(bzt, jnp.concatenate([part[rows] for part in x], axis=0))
        for g in range(ZG):
            part = z[g * GR : (g + 1) * GR]
            out[g, rows, :] = part if first else out[g, rows, :] + part


def quotient_of(layer, code, blur_now):
    lane = iota(code.shape, 1)
    inside = (lane < YQ) | ((lane < TURN) & (layer < VIEWS - 1)) | ((lane >= TURN) & (layer > 0))
    measured = jnp.where(inside, from_code(code) * (1.0 / M_SCALE) + M_MID, 0.0)
    return (measured / jnp.where(inside, blur_now, 1.0)).astype(bf16)


def widened(own, from_left, from_right):
    inverse = 1.0 / E_SCALE
    return jnp.concatenate(
        [from_code(from_left) * inverse, own, from_code(from_right) * inverse], axis=1
    )


def blur_body(own, from_left, from_right, kx, ty, bz, out, field, columns):
    step = pl.program_id(0)

    @pl.when(step == 0)
    def _():
        field[...] = widened(own[...], from_left[...], from_right[...]).astype(bf16)
        blurred_columns(field, kx, columns)

    out[step] = rows_from(blurred(columns[step], ty[step], bz[step]))


def blur(own, from_left, from_right, mats):
    operands = kept([own, from_left, from_right, mats[0], mats[2], mats[4]])
    return pl.pallas_call(
        blur_body,
        grid=(VIEWS,),
        out_shape=pltpu.VMEM((VIEWS, ROWS, YE), f32),
        in_specs=[KEPT] * len(operands),
        out_specs=KEPT,
        scratch_shapes=[pltpu.VMEM((ZG, EXR, YE), bf16), pltpu.VMEM((VIEWS, ROWS, YE), bf16)],
        compiler_params=params(),
        cost_estimate=cost(7e9, 1.6e7),
    )(*operands)


def choose(step, codes, code):
    for i, parts in enumerate(codes):

        @pl.when(step == i)
        def _():
            at = 0
            for part in parts:
                rows = slice(at, at + part.shape[0])
                code[rows, :] = part[...]
                at += part.shape[0]


def grouped(refs, layout):
    refs = iter(refs)
    return [[next(refs) for _ in range(n)] for n in layout]


def mirror_body(views, layout, first, last, place, *rest):
    rest = list(rest)
    before = None if first else rest.pop(0)
    codes, rest = grouped(rest, layout), rest[sum(layout) :]
    blur_ref, kxt, tyt, bzt, total = rest[:5]
    code = rest[-1]
    step = pl.program_id(0)
    view = views[0] + (views[-1] - views[0]) * step
    choose(step, codes, code)
    if not first:

        @pl.when(step == 0)
        def _():
            total[...] = before[...]

    quotient = quotient_of(place[1], code[...], blur_ref[view])
    mirrored(quotient, kxt[view], tyt[view], bzt[view], total, first)
    if last:

        @pl.when(step == pl.num_programs(0) - 1)
        def _():
            left, right = rest[5:7]
            send(left, flat(total[:, : EXR // 2]))
            send(right, flat(total[:, EXR // 2 :]))


def mirror(place, before, codes, views, blur_all, mats, last):
    first = before is None
    layout = tuple(len(parts) for parts in codes)
    columns = jax.ShapeDtypeStruct((ZG * EXR // 2 + 16, YE), i16)
    operands = [] if first else [before]
    operands += [part for parts in codes for part in parts]
    operands = kept(operands + [blur_all, mats[1], mats[3], mats[5]])
    return pl.pallas_call(
        functools.partial(mirror_body, views, layout, first, last),
        grid=(len(views),),
        out_shape=(pltpu.VMEM((ZG, EXR, YE), f32),) + (columns,) * (2 * last),
        in_specs=[pl.BlockSpec(memory_space=pltpu.SMEM)] + [KEPT] * len(operands),
        out_specs=(KEPT,) * (1 + 2 * last),
        scratch_shapes=[pltpu.VMEM((ROWS, YE), i16)],
        compiler_params=params(),
        cost_estimate=cost(2e9 * len(views), 8e6 * len(views)),
    )(place, *operands)


def second_body(layout, place, own, e_left, e_right, total, x_left, x_right, *rest):
    codes, rest = grouped(rest, layout), rest[sum(layout) :]
    kx, kxt, ty, tyt, bz, bzt = rest[:6]
    estimate, center, left, right, field, columns, acc, code = rest[6:]
    step = pl.program_id(0)
    edge = MARGIN * ZI
    middle = EXR // 2

    @pl.when(step == 0)
    def _():
        start = widened(own[...], e_left[...], e_right[...]) * (1.0 / VIEWS)
        for half, came in enumerate((x_left, x_right)):
            rows = slice(half * middle, (half + 1) * middle)
            now = start[:, rows] * (total[:, rows] + lane_value(came).reshape(ZG, middle, YE))
            field[:, rows] = now.astype(bf16)
            inner = now[:, edge:] if half == 0 else now[:, : middle - edge]
            estimate[:, half * edge : (half + 1) * edge] = inner[:, :, :YQ]
        blurred_columns(field, kx, columns)
        acc[...] = jnp.zeros_like(acc)

    choose(step, codes, code)
    blur_now = rows_from(blurred(columns[step], ty[step], bz[step]))
    quotient = quotient_of(place[1], code[...], blur_now)
    mirrored(quotient, kxt[step], tyt[step, :, :YQ], bzt[step], acc, False)

    @pl.when(step == pl.num_programs(0) - 1)
    def _():
        center[...] = acc[:, edge : edge + XR, :]
        send(left, flat(acc[:, :edge, :]))
        send(right, flat(acc[:, edge + XR :, :]))


def second(place, own, e_left, e_right, total, x_left, x_right, codes, mats):
    columns = jax.ShapeDtypeStruct((ZG * MARGIN * ZI + 16, YQ), i16)
    cell_shape = pltpu.VMEM((ZG, XR, YQ), f32)
    layout = tuple(len(parts) for parts in codes)
    operands = [own, e_left, e_right, total, x_left, x_right]
    operands += [part for parts in codes for part in parts] + list(mats)
    operands = kept(operands)
    return pl.pallas_call(
        functools.partial(second_body, layout),
        grid=(VIEWS,),
        out_shape=(cell_shape, cell_shape, columns, columns),
        in_specs=[pl.BlockSpec(memory_space=pltpu.SMEM)] + [KEPT] * len(operands),
        out_specs=(KEPT,) * 4,
        scratch_shapes=[
            pltpu.VMEM((ZG, EXR, YE), bf16),
            pltpu.VMEM((VIEWS, ROWS, YE), bf16),
            pltpu.VMEM((ZG, EXR, YQ), f32),
            pltpu.VMEM((ROWS, YE), i16),
        ],
        compiler_params=params(),
        cost_estimate=cost(1.6e10, 4e7),
    )(place, *operands)


def finish_body(estimate, total, x_left, x_right, low, high):
    middle = XR // 2
    a = total[:, :middle] + lane_value(x_left).reshape(ZG, middle, YQ)
    b = total[:, middle:] + lane_value(x_right).reshape(ZG, middle, YQ)
    send(low, flat(estimate[:, :middle] * a * (1.0 / VIEWS)))
    send(high, flat(estimate[:, middle:] * b * (1.0 / VIEWS)))


def finish(estimate, total, x_left, x_right):
    half = jax.ShapeDtypeStruct((ROWS // 2 + 16, YQ), i16)
    return pl.pallas_call(
        finish_body,
        out_shape=(half, half),
        compiler_params=params(),
        cost_estimate=cost(5e6, 4e6),
    )(*kept([estimate, total, x_left, x_right]))


def spread_out(codes, scratch, store):
    middle = XR // 2
    for half in range(2):
        value = lane_value(codes[half])
        for c in range(2):
            scratch[half, c] = value[:, c * 128 : (c + 1) * 128]
            for z in range(NZ):
                rows = pl.ds(z // ZI * middle + z % ZI, BX // 2, stride=ZI)
                store(z, half, c, scratch[half, c, rows, :])


def gather_body(place, *rest):
    codes, out, scratch = rest[: 2 * VIEWS - 2], rest[2 * VIEWS - 2], rest[2 * VIEWS - 1]
    for i, r in enumerate((0, 1, 3)):
        at = lax.rem(place[1] + VIEWS - r, VIEWS) * YQ

        def store(z, half, c, value):
            lanes = pl.ds(pl.multiple_of(at + c * 128, 128), 128)
            out[z, half * BX // 2 : (half + 1) * BX // 2, lanes] = value

        spread_out(codes[2 * i : 2 * i + 2], scratch.at[i], store)


def gathered(place, codes):
    return pl.pallas_call(
        gather_body,
        out_shape=jax.ShapeDtypeStruct((NZ, BX, VIEWS * YQ), f32),
        in_specs=[pl.BlockSpec(memory_space=pltpu.SMEM)] + [KEPT] * len(codes),
        scratch_shapes=[pltpu.VMEM((VIEWS - 1, 2, 2, ROWS // 2, 128), f32)],
        compiler_params=params(),
        cost_estimate=cost(3e6, 6e6),
    )(place, *kept(codes))


def complete_body(place, low, high, _, out, scratch, quarter, sem):
    def store(z, half, c, value):
        quarter[z, half * BX // 2 : (half + 1) * BX // 2, c * 128 : (c + 1) * 128] = value

    spread_out((low, high), scratch, store)
    at = pl.multiple_of(lax.rem(place[1] + 2, VIEWS) * YQ, YQ)
    move = pltpu.make_async_copy(quarter, out.at[:, :, pl.ds(at, YQ)], sem)
    move.start()
    move.wait()


def completed(place, low, high, out):
    anywhere = pl.BlockSpec(memory_space=pl.ANY)
    vmem = pl.BlockSpec(memory_space=pltpu.VMEM)
    return pl.pallas_call(
        complete_body,
        out_shape=jax.ShapeDtypeStruct(out.shape, f32),
        in_specs=[pl.BlockSpec(memory_space=pltpu.SMEM), vmem, vmem, anywhere],
        out_specs=anywhere,
        input_output_aliases={3: 0},
        scratch_shapes=[
            pltpu.VMEM((2, 2, ROWS // 2, 128), f32),
            pltpu.VMEM((NZ, BX, YQ), f32),
            pltpu.SemaphoreType.DMA,
        ],
        compiler_params=params(),
        cost_estimate=cost(1e6, 2e6),
    )(place, *kept([low, high]), out)


def per_device(view_tiles, route_block, route_column, psf_taps, start_estimate):
    groups = lax.axis_size("block")
    cap = max(2, (2 * BX + groups - 1) // groups)
    me, layer = lax.axis_index("block"), lax.axis_index("view")
    place = jnp.stack([me, layer]).astype(i32)

    def around(x, shift):
        return lax.ppermute(x, "view", [(i, (i + shift) % VIEWS) for i in range(VIEWS)])

    def shifted(x, shift):
        pairs = [(i, i + shift) for i in range(groups) if 0 <= i + shift < groups]
        return lax.ppermute(x, "block", pairs)

    outgoing = pack(cap, groups, route_block[0], route_column[0], view_tiles[0])
    arrived = lax.all_to_all(outgoing, "block", split_axis=0, concat_axis=0, tiled=True)

    psf, start_estimate, _ = lax.optimization_barrier((psf_taps[0], start_estimate, outgoing))
    kernel = psf / jnp.sum(psf, axis=1, keepdims=True)
    kernel = kernel.astype(bf16).astype(f32)
    taps = [kernel] + [around(kernel, r) for r in range(1, VIEWS)]
    own, to_left, to_right = cell(place, start_estimate)
    e_left, e_right = shifted(to_right, 1), shifted(to_left, -1)

    codes = unpack(cap, place, arrived)
    own, taps, codes = lax.optimization_barrier((own, taps, codes))
    low_on, high_on = around(codes[2], 1), around(codes[3], -1)
    codes = [
        [codes[0]],
        [around(codes[1], 1)],
        [around(low_on, 1), around(high_on, -1)],
        [around(codes[4], -1)],
    ]
    mats = bands(jnp.stack(taps).reshape(VIEWS, 3 * TAPS))
    blur_all = blur(own, e_left, e_right, mats)
    (total,) = mirror(place, None, codes[:1], [0], blur_all, mats, False)
    (total,) = mirror(place, total, [codes[1], codes[3]], [1, 3], blur_all, mats, False)
    total, left, right = mirror(place, total, codes[2:3], [2], blur_all, mats, True)
    x_left, x_right = shifted(right, 1), shifted(left, -1)
    estimate, center, left, right = second(
        place, own, e_left, e_right, total, x_left, x_right, codes, mats
    )
    x_left, x_right = shifted(right, 1), shifted(left, -1)
    low, high = finish(estimate, center, x_left, x_right)
    low_after, high_before = around(low, -1), around(high, 1)
    high_after, low_before = around(high, -1), around(low, 1)
    low_across, high_across = around(low_after, -1), around(high_before, 1)
    out = gathered(place, [low, high, low_before, high_before, low_after, high_after])
    return completed(place, low_across, high_across, out)


def solution(mesh):
    placed = (
        P("view", "block", None, None),
        P("view", "block"),
        P("view", "block"),
        P("view", None, None),
        P(None, "block", None),
    )
    return jax.shard_map(
        per_device, mesh=mesh, in_specs=placed, out_specs=P(None, "block", None), check_vma=False
    )
```

```python
import functools

import jax
import jax.numpy as jnp
import numpy as np
from jax import lax
from jax.experimental import pallas as pl
from jax.experimental.pallas import tpu as pltpu
from jax.sharding import PartitionSpec as P

ITERS = 2
TAPS = 31
HALF = 15
VIEWS = 4
NZ = 24
BX = 32
MARGIN = 16
EX = BX + 2 * MARGIN
YQ = 256
YE = 384
TURN = 320
ROWS = BX * NZ
ZI = 8
ZG = NZ // ZI
XR = BX * ZI
EXR = EX * ZI
GX = 8
GR = GX * ZI
ZR = GX * NZ
FULL = 32700.0
STEPS = 128.0
LN2 = float(np.log(2.0))
M_MID, M_SCALE = 2.125, 32767.0 / 1.875
E_SCALE = 32767.0 / 2.0
VMEM = 28 * 1024 * 1024

f32, bf16, i32, i16 = jnp.float32, jnp.bfloat16, jnp.int32, jnp.int16


def params(limit=VMEM):
    return pltpu.CompilerParams(vmem_limit_bytes=limit)


KEPT = pl.BlockSpec(memory_space=pltpu.VMEM)


def kept(operands):
    return [pltpu.with_memory_space_constraint(x, pltpu.VMEM) for x in operands]


def cost(flops, moved):
    return pl.CostEstimate(flops=int(flops), bytes_accessed=int(moved), transcendentals=0)


def dot(a, b):
    return jnp.dot(a, b, preferred_element_type=f32)


def to_code(x):
    return jnp.floor(x + 0.5).astype(i32).astype(i16)


def from_code(c):
    return c.astype(i32).astype(f32)


def scale_steps(top):
    return jnp.ceil(jnp.log(jnp.maximum(top, 1e-30)) * (STEPS / LN2))


def lane_code(value):
    k = scale_steps(jnp.max(jnp.abs(value), axis=0, keepdims=True))
    code = to_code(value * (jnp.exp(k * (-LN2 / STEPS)) * FULL))
    return code, jnp.broadcast_to(k, (16, value.shape[1])).astype(i32).astype(i16)


def lane_value(ref):
    n = ref.shape[0] - 16
    k = from_code(ref[n:])[0:1]
    return from_code(ref[:n]) * (jnp.exp(k * (LN2 / STEPS)) * (1.0 / FULL))


def send(ref, value):
    n = value.shape[0]
    ref[:n], ref[n:] = lane_code(value)


def margin_lanes(shape):
    lane = lax.broadcasted_iota(i32, shape, 1)
    return (lane < 32) | (lane >= 96)


def send_wide(ref, value):
    n = value.shape[0]
    k = scale_steps(jnp.max(jnp.abs(value), axis=0, keepdims=True))
    scaled = value * (jnp.exp(k * (-LN2 / STEPS)) * FULL)
    ref[:n] = to_code(scaled[:, :YQ])
    first, second = scaled[: n // 2, YQ:], scaled[n // 2 :, YQ:]
    shared = jnp.where(margin_lanes(first.shape), first, pltpu.roll(second, 64, 1))
    shared = jnp.concatenate([shared[: n // 4], shared[n // 4 :]], axis=1)
    ref[n : n + n // 4] = to_code(shared)
    k = jnp.concatenate([k[:, :YQ], k[:, YQ:], k[:, YQ:]], axis=1)
    k = jnp.broadcast_to(k, (16, 2 * YQ)).astype(i32).astype(i16)
    ref[n + n // 4 : n + n // 4 + 16] = k[:, :YQ]
    ref[n + n // 4 + 16 :] = k[:, YQ:]


def wide_rows(n):
    return n + n // 4 + 32


def wide_value(ref):
    n = (ref.shape[0] - 32) * 4 // 5
    at = n + n // 4
    center = from_code(ref[:n]) * (jnp.exp(from_code(ref[at : at + 16])[0:1] * (LN2 / STEPS)) / FULL)
    shared = from_code(ref[n:at])
    shared = jnp.concatenate([shared[:, :128], shared[:, 128:]], axis=0)
    ours = margin_lanes(shared.shape)
    first = jnp.where(ours, shared, 0.0)
    second = pltpu.roll(jnp.where(ours, 0.0, shared), 64, 1)
    k = from_code(ref[at + 16 :])[0:1, :128]
    ends = jnp.concatenate([first, second], axis=0) * (jnp.exp(k * (LN2 / STEPS)) / FULL)
    return jnp.concatenate([center, ends], axis=1)


def flat(x):
    return x.reshape(x.shape[0] * x.shape[1], x.shape[2])


def send_sides(encode, place, first, second, left, right):
    even = lax.rem(place[0], 2) == 0

    @pl.when(even)
    def _():
        encode(first, left)
        encode(second, right)

    @pl.when(jnp.logical_not(even))
    def _():
        encode(first, right)
        encode(second, left)


def take_sides(place, first, second, sides):
    even = lax.rem(place[0], 2) == 0

    @pl.when(even)
    def _():
        sides[0], sides[1] = first[...], second[...]

    @pl.when(jnp.logical_not(even))
    def _():
        sides[0], sides[1] = second[...], first[...]


LOADS = 4
SLOT = NZ * 8


def pack_body(cap, blocks, columns, tiles, out, labels, count, slots, held, sent, loaded, pushed):
    pieces = tiles.shape[0]
    part = pieces // LOADS
    groups = out.shape[0]

    def load(i):
        rows = pl.ds(i * part, part)
        return pltpu.make_async_copy(tiles.at[rows], held.at[rows], loaded.at[i])

    for i in range(LOADS):
        load(i).start()

    def clear(i, _):
        labels[i] = 0
        return 0

    lax.fori_loop(0, groups * cap, clear, 0)

    def zero(i, _):
        count[i] = 0
        return 0

    lax.fori_loop(0, groups, zero, 0)

    def route(p, _):
        b = blocks[p]
        rank = count[b]
        count[b] = rank + 1
        slot = b * cap + rank
        labels[slot] = columns[p] + 1
        slots[p] = slot
        return 0

    lax.fori_loop(0, pieces, route, 0)
    lane = lax.broadcasted_iota(i32, (16, 128), 1)

    def mark(b, _):
        row = jnp.zeros((16, 128), i32)
        for rank in range(cap):
            row = jnp.where(lane == rank, labels[b * cap + rank], row)
        sent[b, cap * SLOT :, :] = row.astype(f32).astype(bf16)
        return 0

    lax.fori_loop(0, groups, mark, 0)
    def push(b, at, rows, sem):
        part = pl.ds(pl.multiple_of(at, 16), rows)
        return pltpu.make_async_copy(sent.at[b, part, :], out.at[b, part, :], sem)

    def tags():
        rows = pl.ds(cap * SLOT, 16)
        return pltpu.make_async_copy(sent.at[:, rows, :], out.at[:, rows, :], pushed.at[1])

    tags().start()
    for i in range(LOADS):
        load(i).wait()

        def put(p, _):
            slot = slots[p]
            b = slot // cap
            at = (slot - b * cap) * SLOT
            for c in range(8):
                rows = pl.ds(pl.multiple_of(at + 16 * c, 16), 16)
                sent[b, rows, :] = held[p, :16, 128 * c : 128 * (c + 1)]
            for c in range(0, 8, 2):
                rows = pl.ds(pl.multiple_of(at + 128 + 8 * c, 16), 16)
                sent[b, rows, :] = jnp.concatenate(
                    [
                        held[p, 16:, 128 * c : 128 * (c + 1)],
                        held[p, 16:, 128 * (c + 1) : 128 * (c + 2)],
                    ],
                    axis=0,
                )
            push(b, at, SLOT, pushed.at[0]).start()
            return 0

        lax.fori_loop(i * part, (i + 1) * part, put, 0, unroll=2)
    tags().wait()
    if pieces % cap == 0:
        every = pl.ds(0, pieces // cap), pl.ds(0, cap * SLOT)
        pltpu.make_async_copy(sent.at[every], out.at[every], pushed.at[0]).wait()
    else:
        lax.fori_loop(0, pieces, lambda p, _: push(0, 0, SLOT, pushed.at[0]).wait(), None)


def pack(cap, groups, blocks, columns, tiles):
    smem = pl.BlockSpec(memory_space=pltpu.SMEM)
    message = (groups, cap * SLOT + 16, 128)
    return pl.pallas_call(
        functools.partial(pack_body, cap),
        out_shape=pltpu.HBM(message, bf16),
        in_specs=[smem, smem, pl.BlockSpec(memory_space=pltpu.HBM)],
        out_specs=pl.BlockSpec(memory_space=pltpu.HBM),
        scratch_shapes=[
            pltpu.SMEM((groups * cap,), i32),
            pltpu.SMEM((groups,), i32),
            pltpu.SMEM((tiles.shape[0],), i32),
            pltpu.VMEM(tiles.shape, bf16),
            pltpu.VMEM(message, bf16),
            pltpu.SemaphoreType.DMA((LOADS,)),
            pltpu.SemaphoreType.DMA((2,)),
        ],
        compiler_params=params(2 * VMEM),
        cost_estimate=cost(0, 4 * tiles.size),
    )(blocks, columns, pltpu.with_memory_space_constraint(tiles, pltpu.HBM))


PART_VIEWS = (0, 1, 2, 2, 3)
PART_ROWS = (0, 0, 0, ROWS // 2, 0)


def unpack_body(cap, chunk, place, arrived, whole_arrived, *rest):
    outs, (acc, codes, count, marks, table, labels, sem) = rest[: VIEWS + 1], rest[VIEWS + 1 :]
    step = pl.program_id(0)
    layer = place[1]

    @pl.when(step == 0)
    def _():
        fetch = pltpu.make_async_copy(
            whole_arrived.at[:, pl.ds(cap * SLOT, 16), :], marks, sem.at[0]
        )
        fetch.start()
        acc[...] = jnp.zeros_like(acc)

        def zero(i, _):
            count[i] = 0
            return 0

        lax.fori_loop(0, BX, zero, 0)
        fetch.wait()
        ranks = table.shape[0]
        which = jnp.where(iota((ranks, 128), 0) == iota((ranks, 128), 1), 1.0, 0.0)
        lines = jnp.max(marks[...].astype(f32), axis=1)
        found = lax.dot_general(which, lines, (((1,), (1,)), ((), ())), preferred_element_type=f32)
        table[:, : lines.shape[0]] = found.astype(i32)
        move = pltpu.make_async_copy(table, labels, sem.at[1])
        move.start()
        move.wait()

    for j in range(chunk):
        for rank in range(cap):
            label = labels[rank, step * chunk + j]

            @pl.when(label > 0)
            def _():
                col = label - 1
                rows = pl.ds(pl.multiple_of(col * ZI, ZI), ZI)
                tile = arrived[j, rank * SLOT : (rank + 1) * SLOT, :].astype(f32)
                for c in range(8):
                    lanes = slice(128 * c, 128 * (c + 1))
                    acc[0, rows, lanes] += tile[16 * c : 16 * c + 8]
                    acc[1, rows, lanes] += tile[16 * c + 8 : 16 * c + 16]
                    acc[2, rows, lanes] += tile[128 + 8 * c : 136 + 8 * c]
                count[col] += 1

    @pl.when(step == pl.num_programs(0) - 1)
    def _():
        row = lax.broadcasted_iota(i32, (2 * ZI, 128), 0)
        lane = lax.broadcasted_iota(i32, (2 * ZI, 128), 1)

        def pair(i, _):
            first = M_SCALE / jnp.maximum(count[2 * i], 1).astype(f32)
            second = M_SCALE / jnp.maximum(count[2 * i + 1], 1).astype(f32)
            inverse = jnp.where(row < ZI, first, second)
            for g in range(ZG):
                rows = pl.ds(pl.multiple_of(i * 2 * ZI, 2 * ZI), 2 * ZI)
                to = pl.ds(pl.multiple_of(g * XR + i * 2 * ZI, 2 * ZI), 2 * ZI)
                blocks = [
                    acc[g, rows, 128 * c : 128 * (c + 1)] * inverse - M_MID * M_SCALE
                    for c in range(2 * VIEWS)
                ]
                for v in range(VIEWS):
                    after = blocks[min(2 * v + 2, 2 * VIEWS - 1)]
                    before = blocks[max(2 * v - 1, 0)]
                    ends = jnp.where(lane < 64, after, before)
                    code = jnp.concatenate([blocks[2 * v], blocks[2 * v + 1], ends], axis=1)
                    codes[v, to, :] = to_code(code)
            return 0

        lax.fori_loop(0, BX // 2, pair, 0, unroll=4)
        for r, at, out in zip(PART_VIEWS, PART_ROWS, outs):
            out[...] = codes[lax.rem(layer + r, VIEWS), at : at + out.shape[0], :]


def unpack(cap, place, arrived):
    groups = arrived.shape[0]
    chunk = min(32, groups)
    shapes = [(ROWS // PART_VIEWS.count(r), YE) for r in PART_VIEWS]
    smem = pl.BlockSpec(memory_space=pltpu.SMEM)
    return pl.pallas_call(
        functools.partial(unpack_body, cap, chunk),
        grid=(groups // chunk,),
        out_shape=tuple(jax.ShapeDtypeStruct(shape, i16) for shape in shapes),
        in_specs=[
            smem,
            pl.BlockSpec((chunk,) + arrived.shape[1:], lambda s: (s, 0, 0)),
            pl.BlockSpec(memory_space=pl.ANY),
        ],
        out_specs=tuple(pl.BlockSpec(shape, lambda s: (0, 0)) for shape in shapes),
        scratch_shapes=[
            pltpu.VMEM((ZG, XR, VIEWS * YQ), f32),
            pltpu.VMEM((VIEWS, ROWS, YE), i16),
            pltpu.SMEM((BX,), i32),
            pltpu.VMEM((groups, 16, 128), bf16),
            pltpu.VMEM((max(8, cap), 128), i32),
            pltpu.SMEM((max(8, cap), 128), i32),
            pltpu.SemaphoreType.DMA((2,)),
        ],
        compiler_params=params(),
        cost_estimate=cost(arrived.size, 2 * arrived.size),
    )(place, arrived, arrived)


def iota(shape, dim):
    return lax.broadcasted_iota(i32, shape, dim)


def bands_body(taps, kx, kxt, ty, tyt, bz, bzt):
    r = pl.program_id(0)

    def band(distance, axis):
        out = jnp.zeros(distance.shape, f32)
        for t in range(TAPS):
            out = jnp.where(distance == t, taps[r, axis * TAPS + t], out)
        return out

    def circulant(row, n):
        wide = jnp.broadcast_to(row[0:1], (n, row.shape[1]))
        return pltpu.roll(wide, 0, 1, stride=1, stride_axis=0).astype(bf16)

    m = iota((8, EXR), 1)
    aligned = lax.bitwise_and(m, ZI - 1) == 0
    taps_at = band(lax.shift_right_logical(m, 3) - 1, 1)
    kx[r] = circulant(jnp.where(aligned, taps_at, 0.0), XR)
    taps_at = band(lax.shift_right_logical(EXR - m, 3) - 1, 1)
    kxt[r] = circulant(jnp.where(aligned, taps_at, 0.0), EXR)[:, :XR]
    n = iota((8, YE), 1)
    apart = jnp.where(n < YE // 2, n, n - YE)
    ty[r] = circulant(band(HALF - apart, 2), YE)
    back = circulant(band(HALF + apart, 2), YE)
    tyt[r] = back

    def parts(x):
        group = jnp.where(x >= 2 * GR, 2, jnp.where(x >= GR, 1, 0))
        within = x - group * GR
        return group * ZI + lax.bitwise_and(within, ZI - 1), lax.shift_right_logical(within, 3)

    (zr, xr), (zc, xc) = parts(iota((ZR, 1), 0)), parts(iota((1, ZR), 1))
    same = xr == xc
    bz[r] = jnp.where(same, band(zc - zr + HALF, 0), 0.0).astype(bf16)
    bzt[r] = jnp.where(same, band(zr - zc + HALF, 0), 0.0).astype(bf16)


MATS = [(XR, EXR), (EXR, XR), (YE, YE), (YE, YE), (ZR, ZR), (ZR, ZR)]


def bands(taps):
    return pl.pallas_call(
        bands_body,
        grid=(VIEWS,),
        out_shape=tuple(pltpu.VMEM((VIEWS,) + s, bf16) for s in MATS),
        in_specs=[pl.BlockSpec(memory_space=pltpu.SMEM)],
        out_specs=(KEPT,) * len(MATS),
        compiler_params=params(),
        cost_estimate=cost(4e9, 2e7),
    )(taps)


def cell_body(place, start, own, left, right, scratch):
    layer = place[1]
    last = start.shape[2] - 128
    after = jnp.minimum((layer + 1) * YQ, last)
    before = jnp.maximum(layer * YQ - 128, 0)
    lane = iota((BX, 128), 1)
    for z in range(NZ):
        rows = pl.ds(z // ZI * XR + z % ZI, BX, stride=ZI)
        for c in range(2):
            at = pl.multiple_of(layer * YQ + c * 128, 128)
            scratch[c, rows, :] = start[z, :, pl.ds(at, 128)]
        head = start[z, :, pl.ds(pl.multiple_of(after, 128), 128)]
        tail = start[z, :, pl.ds(pl.multiple_of(before, 128), 128)]
        head = jnp.where((lane < TURN - YQ) & (layer < VIEWS - 1), head, 0.0)
        tail = jnp.where((lane >= TURN - YQ) & (layer > 0), tail, 0.0)
        scratch[2, rows, :] = head + tail
    value = jnp.concatenate([scratch[c] for c in range(3)], axis=1)
    own[...] = value.reshape(ZG, XR, YE)
    code = to_code(value * E_SCALE).reshape(ZG, XR, YE)
    left[...] = code[:, : XR // 2]
    right[...] = code[:, XR // 2 :]


def cell(place, start):
    half = jax.ShapeDtypeStruct((ZG, XR // 2, YE), i16)
    return pl.pallas_call(
        cell_body,
        out_shape=(pltpu.VMEM((ZG, XR, YE), f32), half, half),
        in_specs=[
            pl.BlockSpec(memory_space=pltpu.SMEM),
            pl.BlockSpec(memory_space=pltpu.VMEM),
        ],
        scratch_shapes=[pltpu.VMEM((3, ROWS, 128), f32)],
        compiler_params=params(),
        cost_estimate=cost(3e6, 6e6),
    )(place, start)


def blurred_columns(field, kx, out):
    for g in range(ZG):
        x = dot(kx[...].reshape(VIEWS * XR, EXR), field[g]).astype(bf16)
        out[:, g * XR : (g + 1) * XR, :] = x.reshape(VIEWS, XR, YE)


def blurred(x, ty, bz):
    y = dot(x, ty).astype(bf16)
    return [dot(bz, columns_of(y, XR, c)) for c in range(BX // GX)]


def columns_of(rows, stride, c):
    return jnp.concatenate(
        [rows[g * stride + c * GR : g * stride + (c + 1) * GR] for g in range(ZG)], axis=0
    )


def rows_from(groups):
    return jnp.concatenate(
        [part[g * GR : (g + 1) * GR] for g in range(ZG) for part in groups], axis=0
    )


def mirrored(quotient, kxt, tyt, bzt, out, first):
    y = dot(quotient, tyt).astype(bf16)
    x = [dot(kxt, y[g * XR : (g + 1) * XR]).astype(bf16) for g in range(ZG)]
    for c in range(EX // GX):
        rows = slice(c * GR, (c + 1) * GR)
        z = dot(bzt, jnp.concatenate([part[rows] for part in x], axis=0))
        for g in range(ZG):
            part = z[g * GR : (g + 1) * GR]
            out[g, rows, :] = part if first else out[g, rows, :] + part


def quotient_of(layer, code, blur_now):
    lane = iota(code.shape, 1)
    inside = (lane < YQ) | ((lane < TURN) & (layer < VIEWS - 1)) | ((lane >= TURN) & (layer > 0))
    measured = jnp.where(inside, from_code(code) * (1.0 / M_SCALE) + M_MID, 0.0)
    return (measured / jnp.where(inside, blur_now, 1.0)).astype(bf16)


def widened(own, from_left, from_right):
    inverse = 1.0 / E_SCALE
    return jnp.concatenate(
        [from_code(from_left) * inverse, own, from_code(from_right) * inverse], axis=1
    )


def blur_body(own, from_left, from_right, kx, ty, bz, out, field, columns):
    step = pl.program_id(0)

    @pl.when(step == 0)
    def _():
        field[...] = widened(own[...], from_left[...], from_right[...]).astype(bf16)
        blurred_columns(field, kx, columns)

    out[step] = rows_from(blurred(columns[step], ty[step], bz[step]))


def blur(own, from_left, from_right, mats):
    operands = kept([own, from_left, from_right, mats[0], mats[2], mats[4]])
    return pl.pallas_call(
        blur_body,
        grid=(VIEWS,),
        out_shape=pltpu.VMEM((VIEWS, ROWS, YE), f32),
        in_specs=[KEPT] * len(operands),
        out_specs=KEPT,
        scratch_shapes=[pltpu.VMEM((ZG, EXR, YE), bf16), pltpu.VMEM((VIEWS, ROWS, YE), bf16)],
        compiler_params=params(),
        cost_estimate=cost(7e9, 1.6e7),
    )(*operands)


def joined(parts):
    return jnp.concatenate([part[...] for part in parts], axis=0)


def grouped(refs, layout):
    refs = iter(refs)
    return [[next(refs) for _ in range(n)] for n in layout]


def mirror_body(views, layout, first, last, place, *rest):
    rest = list(rest)
    before = None if first else rest.pop(0)
    codes, rest = grouped(rest, layout), rest[sum(layout) :]
    blur_ref, kxt, tyt, bzt, total = rest[:5]
    if not first:
        total[...] = before[...]
    for r, parts in zip(views, codes):
        quotient = quotient_of(place[1], joined(parts), blur_ref[r])
        mirrored(quotient, kxt[r], tyt[r], bzt[r], total, first)
    if last:
        left, right = flat(total[:, : EXR // 2]), flat(total[:, EXR // 2 :])
        send_sides(send_wide, place, rest[5], rest[6], left, right)


def mirror(place, before, codes, views, blur_all, mats, last):
    first = before is None
    layout = tuple(len(parts) for parts in codes)
    columns = jax.ShapeDtypeStruct((wide_rows(ZG * EXR // 2), YQ), i16)
    operands = [] if first else [before]
    operands += [part for parts in codes for part in parts]
    operands = kept(operands + [blur_all, mats[1], mats[3], mats[5]])
    return pl.pallas_call(
        functools.partial(mirror_body, views, layout, first, last),
        out_shape=(pltpu.VMEM((ZG, EXR, YE), f32),) + (columns,) * (2 * last),
        in_specs=[pl.BlockSpec(memory_space=pltpu.SMEM)] + [KEPT] * len(operands),
        out_specs=(KEPT,) * (1 + 2 * last),
        compiler_params=params(),
        cost_estimate=cost(2e9 * len(views), 8e6 * len(views)),
    )(place, *operands)


def second_body(layout, place, own, e_left, e_right, total, x_first, x_second, *rest):
    codes, rest = grouped(rest, layout), rest[sum(layout) :]
    kx, kxt, ty, tyt, bz, bzt = rest[:6]
    estimate, center, first, second, field, columns, acc, sides = rest[6:]
    take_sides(place, x_first, x_second, sides)
    edge = MARGIN * ZI
    middle = EXR // 2
    start = widened(own[...], e_left[...], e_right[...]) * (1.0 / VIEWS)
    for half in range(2):
        came = sides.at[half]
        rows = slice(half * middle, (half + 1) * middle)
        now = start[:, rows] * (total[:, rows] + wide_value(came).reshape(ZG, middle, YE))
        field[:, rows] = now.astype(bf16)
        inner = now[:, edge:] if half == 0 else now[:, : middle - edge]
        estimate[:, half * edge : (half + 1) * edge] = inner[:, :, :YQ]
    blurred_columns(field, kx, columns)
    for r in range(VIEWS):
        blur_now = rows_from(blurred(columns[r], ty[r], bz[r]))
        quotient = quotient_of(place[1], joined(codes[r]), blur_now)
        mirrored(quotient, kxt[r], tyt[r, :, :YQ], bzt[r], acc, r == 0)
    center[...] = acc[:, edge : edge + XR, :]
    send_sides(send, place, first, second, flat(acc[:, :edge, :]), flat(acc[:, edge + XR :, :]))


def second(place, own, e_left, e_right, total, x_first, x_second, codes, mats):
    columns = jax.ShapeDtypeStruct((ZG * MARGIN * ZI + 16, YQ), i16)
    cell_shape = pltpu.VMEM((ZG, XR, YQ), f32)
    layout = tuple(len(parts) for parts in codes)
    operands = [own, e_left, e_right, total, x_first, x_second]
    operands += [part for parts in codes for part in parts] + list(mats)
    operands = kept(operands)
    return pl.pallas_call(
        functools.partial(second_body, layout),
        out_shape=(cell_shape, cell_shape, columns, columns),
        in_specs=[pl.BlockSpec(memory_space=pltpu.SMEM)] + [KEPT] * len(operands),
        out_specs=(KEPT,) * 4,
        scratch_shapes=[
            pltpu.VMEM((ZG, EXR, YE), bf16),
            pltpu.VMEM((VIEWS, ROWS, YE), bf16),
            pltpu.VMEM((ZG, EXR, YQ), f32),
            pltpu.VMEM((2,) + x_first.shape, i16),
        ],
        compiler_params=params(),
        cost_estimate=cost(1.6e10, 4e7),
    )(place, *operands)


def finish_body(place, estimate, total, x_first, x_second, low, high, sides):
    take_sides(place, x_first, x_second, sides)
    middle = XR // 2
    a = total[:, :middle] + lane_value(sides.at[0]).reshape(ZG, middle, YQ)
    b = total[:, middle:] + lane_value(sides.at[1]).reshape(ZG, middle, YQ)
    send(low, flat(estimate[:, :middle] * a * (1.0 / VIEWS)))
    send(high, flat(estimate[:, middle:] * b * (1.0 / VIEWS)))


def finish(place, estimate, total, x_first, x_second):
    half = jax.ShapeDtypeStruct((ROWS // 2 + 16, YQ), i16)
    return pl.pallas_call(
        finish_body,
        out_shape=(half, half),
        in_specs=[pl.BlockSpec(memory_space=pltpu.SMEM)] + [KEPT] * 4,
        out_specs=(KEPT, KEPT),
        scratch_shapes=[pltpu.VMEM((2,) + x_first.shape, i16)],
        compiler_params=params(),
        cost_estimate=cost(5e6, 4e6),
    )(place, *kept([estimate, total, x_first, x_second]))


def spread_out(codes, scratch, store):
    middle = XR // 2
    for half in range(2):
        value = lane_value(codes[half])
        for c in range(2):
            scratch[half, c] = value[:, c * 128 : (c + 1) * 128]
            for z in range(NZ):
                rows = pl.ds(z // ZI * middle + z % ZI, BX // 2, stride=ZI)
                store(z, half, c, scratch[half, c, rows, :])


def gather_body(place, *rest):
    codes, out, scratch = rest[: 2 * VIEWS - 2], rest[2 * VIEWS - 2], rest[2 * VIEWS - 1]
    for i, r in enumerate((0, 1, 3)):
        at = lax.rem(place[1] + VIEWS - r, VIEWS) * YQ

        def store(z, half, c, value):
            lanes = pl.ds(pl.multiple_of(at + c * 128, 128), 128)
            out[z, half * BX // 2 : (half + 1) * BX // 2, lanes] = value

        spread_out(codes[2 * i : 2 * i + 2], scratch.at[i], store)


def gathered(place, codes):
    return pl.pallas_call(
        gather_body,
        out_shape=jax.ShapeDtypeStruct((NZ, BX, VIEWS * YQ), f32),
        in_specs=[pl.BlockSpec(memory_space=pltpu.SMEM)] + [KEPT] * len(codes),
        scratch_shapes=[pltpu.VMEM((VIEWS - 1, 2, 2, ROWS // 2, 128), f32)],
        compiler_params=params(),
        cost_estimate=cost(3e6, 6e6),
    )(place, *kept(codes))


def complete_body(place, low, high, _, out, scratch, quarter, sem):
    def store(z, half, c, value):
        quarter[z, half * BX // 2 : (half + 1) * BX // 2, c * 128 : (c + 1) * 128] = value

    spread_out((low, high), scratch, store)
    at = pl.multiple_of(lax.rem(place[1] + 2, VIEWS) * YQ, YQ)
    move = pltpu.make_async_copy(quarter, out.at[:, :, pl.ds(at, YQ)], sem)
    move.start()
    move.wait()


def completed(place, low, high, out):
    anywhere = pl.BlockSpec(memory_space=pl.ANY)
    vmem = pl.BlockSpec(memory_space=pltpu.VMEM)
    return pl.pallas_call(
        complete_body,
        out_shape=jax.ShapeDtypeStruct(out.shape, f32),
        in_specs=[pl.BlockSpec(memory_space=pltpu.SMEM), vmem, vmem, anywhere],
        out_specs=anywhere,
        input_output_aliases={3: 0},
        scratch_shapes=[
            pltpu.VMEM((2, 2, ROWS // 2, 128), f32),
            pltpu.VMEM((NZ, BX, YQ), f32),
            pltpu.SemaphoreType.DMA,
        ],
        compiler_params=params(),
        cost_estimate=cost(1e6, 2e6),
    )(place, *kept([low, high]), out)


def per_device(view_tiles, route_block, route_column, psf_taps, start_estimate):
    groups = lax.axis_size("block")
    cap = max(2, (2 * BX + groups - 1) // groups)
    me, layer = lax.axis_index("block"), lax.axis_index("view")
    place = jnp.stack([me, layer]).astype(i32)

    def around(x, shift):
        return lax.ppermute(x, "view", [(i, (i + shift) % VIEWS) for i in range(VIEWS)])

    def shifted(x, shift):
        pairs = [(i, i + shift) for i in range(groups) if 0 <= i + shift < groups]
        return lax.ppermute(x, "block", pairs)

    def swapped(x, start):
        pairs = []
        for i in range(start, groups - 1, 2):
            pairs += [(i, i + 1), (i + 1, i)]
        return lax.ppermute(x, "block", pairs) if pairs else jnp.zeros_like(x)

    outgoing = pack(cap, groups, route_block[0], route_column[0], view_tiles[0])
    arrived = lax.all_to_all(outgoing, "block", split_axis=0, concat_axis=0, tiled=True)

    psf, start_estimate, _ = lax.optimization_barrier((psf_taps[0], start_estimate, outgoing))
    kernel = psf / jnp.sum(psf, axis=1, keepdims=True)
    kernel = kernel.astype(bf16).astype(f32)
    taps = [kernel] + [around(kernel, r) for r in range(1, VIEWS)]
    own, to_left, to_right = cell(place, start_estimate)
    e_left, e_right = shifted(to_right, 1), shifted(to_left, -1)

    codes = unpack(cap, place, arrived)
    own, taps, codes = lax.optimization_barrier((own, taps, codes))
    low_on, high_on = around(codes[2], 1), around(codes[3], -1)
    codes = [
        [codes[0]],
        [around(codes[1], 1)],
        [around(low_on, 1), around(high_on, -1)],
        [around(codes[4], -1)],
    ]
    mats = bands(jnp.stack(taps).reshape(VIEWS, 3 * TAPS))
    blur_all = blur(own, e_left, e_right, mats)
    (total,) = mirror(place, None, codes[:1], [0], blur_all, mats, False)
    (total,) = mirror(place, total, [codes[1], codes[3]], [1, 3], blur_all, mats, False)
    total, first, second_part = mirror(place, total, codes[2:3], [2], blur_all, mats, True)
    x_first, x_second = swapped(first, 1), swapped(second_part, 0)
    estimate, center, first, second_part = second(
        place, own, e_left, e_right, total, x_first, x_second, codes, mats
    )
    x_first, x_second = swapped(first, 1), swapped(second_part, 0)
    low, high = finish(place, estimate, center, x_first, x_second)
    low_after, high_before = around(low, -1), around(high, 1)
    high_after, low_before = around(high, -1), around(low, 1)
    low_across, high_across = around(low_after, -1), around(high_before, 1)
    out = gathered(place, [low, high, low_before, high_before, low_after, high_after])
    return completed(place, low_across, high_across, out)


def solution(mesh):
    placed = (
        P("view", "block", None, None),
        P("view", "block"),
        P("view", "block"),
        P("view", None, None),
        P(None, "block", None),
    )
    return jax.shard_map(
        per_device, mesh=mesh, in_specs=placed, out_specs=P(None, "block", None), check_vma=False
    )
```

```python
import functools

import jax
import jax.numpy as jnp
import numpy as np
from jax import lax
from jax.experimental import pallas as pl
from jax.experimental.pallas import tpu as pltpu
from jax.sharding import PartitionSpec as P

ITERS = 2
TAPS = 31
HALF = 15
VIEWS = 4
NZ = 24
BX = 32
MARGIN = 16
EX = BX + 2 * MARGIN
YQ = 256
YE = 384
TURN = 320
ROWS = BX * NZ
ZI = 8
ZG = NZ // ZI
XR = BX * ZI
EXR = EX * ZI
GX = 8
GR = GX * ZI
ZR = GX * NZ
FULL = 32700.0
STEPS = 128.0
LN2 = float(np.log(2.0))
M_MID, M_SCALE = 2.125, 32767.0 / 1.875
E_SCALE = 32767.0 / 2.0
VMEM = 28 * 1024 * 1024

f32, bf16, i32, i16 = jnp.float32, jnp.bfloat16, jnp.int32, jnp.int16


def params(limit=VMEM):
    return pltpu.CompilerParams(vmem_limit_bytes=limit)


KEPT = pl.BlockSpec(memory_space=pltpu.VMEM)


def kept(operands):
    return [pltpu.with_memory_space_constraint(x, pltpu.VMEM) for x in operands]


def cost(flops, moved):
    return pl.CostEstimate(flops=int(flops), bytes_accessed=int(moved), transcendentals=0)


def dot(a, b):
    return jnp.dot(a, b, preferred_element_type=f32)


def to_code(x):
    return jnp.floor(x + 0.5).astype(i32).astype(i16)


def from_code(c):
    return c.astype(i32).astype(f32)


def scale_steps(top):
    return jnp.ceil(jnp.log(jnp.maximum(top, 1e-30)) * (STEPS / LN2))


def lane_code(value):
    k = scale_steps(jnp.max(jnp.abs(value), axis=0, keepdims=True))
    code = to_code(value * (jnp.exp(k * (-LN2 / STEPS)) * FULL))
    return code, jnp.broadcast_to(k, (16, value.shape[1])).astype(i32).astype(i16)


def lane_value(ref):
    n = ref.shape[0] - 16
    k = from_code(ref[n:])[0:1]
    return from_code(ref[:n]) * (jnp.exp(k * (LN2 / STEPS)) * (1.0 / FULL))


def send(ref, value):
    n = value.shape[0]
    ref[:n], ref[n:] = lane_code(value)


def margin_lanes(shape):
    lane = lax.broadcasted_iota(i32, shape, 1)
    return (lane < 32) | (lane >= 96)


def send_wide(ref, value):
    n = value.shape[0]
    k = scale_steps(jnp.max(jnp.abs(value), axis=0, keepdims=True))
    scaled = value * (jnp.exp(k * (-LN2 / STEPS)) * FULL)
    ref[:n] = to_code(scaled[:, :YQ])
    first, second = scaled[: n // 2, YQ:], scaled[n // 2 :, YQ:]
    shared = jnp.where(margin_lanes(first.shape), first, pltpu.roll(second, 64, 1))
    shared = jnp.concatenate([shared[: n // 4], shared[n // 4 :]], axis=1)
    ref[n : n + n // 4] = to_code(shared)
    k = jnp.concatenate([k[:, :YQ], k[:, YQ:], k[:, YQ:]], axis=1)
    k = jnp.broadcast_to(k, (16, 2 * YQ)).astype(i32).astype(i16)
    ref[n + n // 4 : n + n // 4 + 16] = k[:, :YQ]
    ref[n + n // 4 + 16 :] = k[:, YQ:]


def wide_rows(n):
    return n + n // 4 + 32


def wide_value(ref):
    n = (ref.shape[0] - 32) * 4 // 5
    at = n + n // 4
    center = from_code(ref[:n]) * (jnp.exp(from_code(ref[at : at + 16])[0:1] * (LN2 / STEPS)) / FULL)
    shared = from_code(ref[n:at])
    shared = jnp.concatenate([shared[:, :128], shared[:, 128:]], axis=0)
    ours = margin_lanes(shared.shape)
    first = jnp.where(ours, shared, 0.0)
    second = pltpu.roll(jnp.where(ours, 0.0, shared), 64, 1)
    k = from_code(ref[at + 16 :])[0:1, :128]
    ends = jnp.concatenate([first, second], axis=0) * (jnp.exp(k * (LN2 / STEPS)) / FULL)
    return jnp.concatenate([center, ends], axis=1)


def flat(x):
    return x.reshape(x.shape[0] * x.shape[1], x.shape[2])


def send_sides(encode, place, first, second, left, right, sides):
    encode(sides.at[0], left)
    encode(sides.at[1], right)
    even = lax.rem(place[0], 2) == 0

    @pl.when(even)
    def _():
        first[...], second[...] = sides[0], sides[1]

    @pl.when(jnp.logical_not(even))
    def _():
        first[...], second[...] = sides[1], sides[0]


def take_sides(place, first, second, sides):
    even = lax.rem(place[0], 2) == 0

    @pl.when(even)
    def _():
        sides[0], sides[1] = first[...], second[...]

    @pl.when(jnp.logical_not(even))
    def _():
        sides[0], sides[1] = second[...], first[...]


LOADS = 4
SLOT = NZ * 8


def pack_body(cap, blocks, columns, tiles, out, labels, count, slots, held, sent, loaded, pushed):
    pieces = tiles.shape[0]
    part = pieces // LOADS
    groups = out.shape[0]

    def load(i):
        rows = pl.ds(i * part, part)
        return pltpu.make_async_copy(tiles.at[rows], held.at[rows], loaded.at[i])

    for i in range(LOADS):
        load(i).start()

    def clear(i, _):
        labels[i] = 0
        return 0

    lax.fori_loop(0, groups * cap, clear, 0)

    def zero(i, _):
        count[i] = 0
        return 0

    lax.fori_loop(0, groups, zero, 0)

    def route(p, _):
        b = blocks[p]
        rank = count[b]
        count[b] = rank + 1
        slot = b * cap + rank
        labels[slot] = columns[p] + 1
        slots[p] = slot
        return 0

    lax.fori_loop(0, pieces, route, 0)
    lane = lax.broadcasted_iota(i32, (16, 128), 1)

    def mark(b, _):
        row = jnp.zeros((16, 128), i32)
        for rank in range(cap):
            row = jnp.where(lane == rank, labels[b * cap + rank], row)
        sent[b, cap * SLOT :, :] = row.astype(f32).astype(bf16)
        return 0

    lax.fori_loop(0, groups, mark, 0)
    def push(b, at, rows, sem):
        part = pl.ds(pl.multiple_of(at, 16), rows)
        return pltpu.make_async_copy(sent.at[b, part, :], out.at[b, part, :], sem)

    def tags():
        rows = pl.ds(cap * SLOT, 16)
        return pltpu.make_async_copy(sent.at[:, rows, :], out.at[:, rows, :], pushed.at[1])

    tags().start()
    for i in range(LOADS):
        load(i).wait()

        def put(p, _):
            slot = slots[p]
            b = slot // cap
            at = (slot - b * cap) * SLOT
            for c in range(8):
                rows = pl.ds(pl.multiple_of(at + 16 * c, 16), 16)
                sent[b, rows, :] = held[p, :16, 128 * c : 128 * (c + 1)]
            for c in range(0, 8, 2):
                rows = pl.ds(pl.multiple_of(at + 128 + 8 * c, 16), 16)
                sent[b, rows, :] = jnp.concatenate(
                    [
                        held[p, 16:, 128 * c : 128 * (c + 1)],
                        held[p, 16:, 128 * (c + 1) : 128 * (c + 2)],
                    ],
                    axis=0,
                )
            push(b, at, SLOT, pushed.at[0]).start()
            return 0

        lax.fori_loop(i * part, (i + 1) * part, put, 0, unroll=2)
    tags().wait()
    if pieces % cap == 0:
        every = pl.ds(0, pieces // cap), pl.ds(0, cap * SLOT)
        pltpu.make_async_copy(sent.at[every], out.at[every], pushed.at[0]).wait()
    else:
        lax.fori_loop(0, pieces, lambda p, _: push(0, 0, SLOT, pushed.at[0]).wait(), None)


def pack(cap, groups, blocks, columns, tiles):
    smem = pl.BlockSpec(memory_space=pltpu.SMEM)
    message = (groups, cap * SLOT + 16, 128)
    return pl.pallas_call(
        functools.partial(pack_body, cap),
        out_shape=pltpu.HBM(message, bf16),
        in_specs=[smem, smem, pl.BlockSpec(memory_space=pltpu.HBM)],
        out_specs=pl.BlockSpec(memory_space=pltpu.HBM),
        scratch_shapes=[
            pltpu.SMEM((groups * cap,), i32),
            pltpu.SMEM((groups,), i32),
            pltpu.SMEM((tiles.shape[0],), i32),
            pltpu.VMEM(tiles.shape, bf16),
            pltpu.VMEM(message, bf16),
            pltpu.SemaphoreType.DMA((LOADS,)),
            pltpu.SemaphoreType.DMA((2,)),
        ],
        compiler_params=params(2 * VMEM),
        cost_estimate=cost(0, 4 * tiles.size),
    )(blocks, columns, pltpu.with_memory_space_constraint(tiles, pltpu.HBM))


PART_VIEWS = (0, 1, 2, 2, 3)
PART_ROWS = (0, 0, 0, ROWS // 2, 0)


def unpack_body(cap, chunk, place, arrived, whole_arrived, *rest):
    outs, (acc, codes, count, marks, table, labels, sem) = rest[: VIEWS + 1], rest[VIEWS + 1 :]
    step = pl.program_id(0)
    layer = place[1]

    @pl.when(step == 0)
    def _():
        fetch = pltpu.make_async_copy(
            whole_arrived.at[:, pl.ds(cap * SLOT, 16), :], marks, sem.at[0]
        )
        fetch.start()
        acc[...] = jnp.zeros_like(acc)

        def zero(i, _):
            count[i] = 0
            return 0

        lax.fori_loop(0, BX, zero, 0)
        fetch.wait()
        ranks = table.shape[0]
        which = jnp.where(iota((ranks, 128), 0) == iota((ranks, 128), 1), 1.0, 0.0)
        lines = jnp.max(marks[...].astype(f32), axis=1)
        found = lax.dot_general(which, lines, (((1,), (1,)), ((), ())), preferred_element_type=f32)
        table[:, : lines.shape[0]] = found.astype(i32)
        move = pltpu.make_async_copy(table, labels, sem.at[1])
        move.start()
        move.wait()

    def from_source(j, _):
        for rank in range(cap):
            label = labels[rank, step * chunk + j]

            @pl.when(label > 0)
            def _():
                col = label - 1
                rows = pl.ds(pl.multiple_of(col * ZI, ZI), ZI)
                tile = arrived[j, rank * SLOT : (rank + 1) * SLOT, :].astype(f32)
                for c in range(8):
                    lanes = slice(128 * c, 128 * (c + 1))
                    acc[0, rows, lanes] += tile[16 * c : 16 * c + 8]
                    acc[1, rows, lanes] += tile[16 * c + 8 : 16 * c + 16]
                    acc[2, rows, lanes] += tile[128 + 8 * c : 136 + 8 * c]
                count[col] += 1

        return 0

    lax.fori_loop(0, chunk, from_source, 0, unroll=4)

    @pl.when(step == pl.num_programs(0) - 1)
    def _():
        row = lax.broadcasted_iota(i32, (2 * ZI, 128), 0)
        lane = lax.broadcasted_iota(i32, (2 * ZI, 128), 1)

        def pair(i, _):
            first = M_SCALE / jnp.maximum(count[2 * i], 1).astype(f32)
            second = M_SCALE / jnp.maximum(count[2 * i + 1], 1).astype(f32)
            inverse = jnp.where(row < ZI, first, second)
            for g in range(ZG):
                rows = pl.ds(pl.multiple_of(i * 2 * ZI, 2 * ZI), 2 * ZI)
                to = pl.ds(pl.multiple_of(g * XR + i * 2 * ZI, 2 * ZI), 2 * ZI)
                blocks = [
                    acc[g, rows, 128 * c : 128 * (c + 1)] * inverse - M_MID * M_SCALE
                    for c in range(2 * VIEWS)
                ]
                for v in range(VIEWS):
                    after = blocks[min(2 * v + 2, 2 * VIEWS - 1)]
                    before = blocks[max(2 * v - 1, 0)]
                    ends = jnp.where(lane < 64, after, before)
                    code = jnp.concatenate([blocks[2 * v], blocks[2 * v + 1], ends], axis=1)
                    codes[v, to, :] = to_code(code)
            return 0

        lax.fori_loop(0, BX // 2, pair, 0, unroll=2)
        for r, at, out in zip(PART_VIEWS, PART_ROWS, outs):
            out[...] = codes[lax.rem(layer + r, VIEWS), at : at + out.shape[0], :]


def unpack(cap, place, arrived):
    groups = arrived.shape[0]
    chunk = min(32, groups)
    shapes = [(ROWS // PART_VIEWS.count(r), YE) for r in PART_VIEWS]
    smem = pl.BlockSpec(memory_space=pltpu.SMEM)
    return pl.pallas_call(
        functools.partial(unpack_body, cap, chunk),
        grid=(groups // chunk,),
        out_shape=tuple(jax.ShapeDtypeStruct(shape, i16) for shape in shapes),
        in_specs=[
            smem,
            pl.BlockSpec((chunk,) + arrived.shape[1:], lambda s: (s, 0, 0)),
            pl.BlockSpec(memory_space=pl.ANY),
        ],
        out_specs=tuple(pl.BlockSpec(shape, lambda s: (0, 0)) for shape in shapes),
        scratch_shapes=[
            pltpu.VMEM((ZG, XR, VIEWS * YQ), f32),
            pltpu.VMEM((VIEWS, ROWS, YE), i16),
            pltpu.SMEM((BX,), i32),
            pltpu.VMEM((groups, 16, 128), bf16),
            pltpu.VMEM((max(8, cap), 128), i32),
            pltpu.SMEM((max(8, cap), 128), i32),
            pltpu.SemaphoreType.DMA((2,)),
        ],
        compiler_params=params(),
        cost_estimate=cost(arrived.size, 2 * arrived.size),
    )(place, arrived, arrived)


def iota(shape, dim):
    return lax.broadcasted_iota(i32, shape, dim)


def bands_body(taps, kx, kxt, ty, tyt, bz, bzt):
    r = pl.program_id(0)

    def band(distance, axis):
        out = jnp.zeros(distance.shape, f32)
        for t in range(TAPS):
            out = jnp.where(distance == t, taps[r, axis * TAPS + t], out)
        return out

    def circulant(row, n):
        wide = jnp.broadcast_to(row[0:1], (n, row.shape[1]))
        return pltpu.roll(wide, 0, 1, stride=1, stride_axis=0).astype(bf16)

    m = iota((8, EXR), 1)
    aligned = lax.bitwise_and(m, ZI - 1) == 0
    taps_at = band(lax.shift_right_logical(m, 3) - 1, 1)
    kx[r] = circulant(jnp.where(aligned, taps_at, 0.0), XR)
    taps_at = band(lax.shift_right_logical(EXR - m, 3) - 1, 1)
    kxt[r] = circulant(jnp.where(aligned, taps_at, 0.0), EXR)[:, :XR]
    n = iota((8, YE), 1)
    apart = jnp.where(n < YE // 2, n, n - YE)
    ty[r] = circulant(band(HALF - apart, 2), YE)
    back = circulant(band(HALF + apart, 2), YE)
    tyt[r] = back

    def parts(x):
        group = jnp.where(x >= 2 * GR, 2, jnp.where(x >= GR, 1, 0))
        within = x - group * GR
        return group * ZI + lax.bitwise_and(within, ZI - 1), lax.shift_right_logical(within, 3)

    (zr, xr), (zc, xc) = parts(iota((ZR, 1), 0)), parts(iota((1, ZR), 1))
    same = xr == xc
    bz[r] = jnp.where(same, band(zc - zr + HALF, 0), 0.0).astype(bf16)
    bzt[r] = jnp.where(same, band(zr - zc + HALF, 0), 0.0).astype(bf16)


MATS = [(XR, EXR), (EXR, XR), (YE, YE), (YE, YE), (ZR, ZR), (ZR, ZR)]


def bands(taps):
    return pl.pallas_call(
        bands_body,
        grid=(VIEWS,),
        out_shape=tuple(pltpu.VMEM((VIEWS,) + s, bf16) for s in MATS),
        in_specs=[pl.BlockSpec(memory_space=pltpu.SMEM)],
        out_specs=(KEPT,) * len(MATS),
        compiler_params=params(),
        cost_estimate=cost(4e9, 2e7),
    )(taps)


def cell_body(place, start, own, left, right, scratch):
    layer = place[1]
    last = start.shape[2] - 128
    after = jnp.minimum((layer + 1) * YQ, last)
    before = jnp.maximum(layer * YQ - 128, 0)
    lane = iota((BX, 128), 1)
    for z in range(NZ):
        rows = pl.ds(z // ZI * XR + z % ZI, BX, stride=ZI)
        for c in range(2):
            at = pl.multiple_of(layer * YQ + c * 128, 128)
            scratch[c, rows, :] = start[z, :, pl.ds(at, 128)]
        head = start[z, :, pl.ds(pl.multiple_of(after, 128), 128)]
        tail = start[z, :, pl.ds(pl.multiple_of(before, 128), 128)]
        head = jnp.where((lane < TURN - YQ) & (layer < VIEWS - 1), head, 0.0)
        tail = jnp.where((lane >= TURN - YQ) & (layer > 0), tail, 0.0)
        scratch[2, rows, :] = head + tail
    value = jnp.concatenate([scratch[c] for c in range(3)], axis=1)
    own[...] = value.reshape(ZG, XR, YE)
    code = to_code(value * E_SCALE).reshape(ZG, XR, YE)
    left[...] = code[:, : XR // 2]
    right[...] = code[:, XR // 2 :]


def cell(place, start):
    half = jax.ShapeDtypeStruct((ZG, XR // 2, YE), i16)
    return pl.pallas_call(
        cell_body,
        out_shape=(pltpu.VMEM((ZG, XR, YE), f32), half, half),
        in_specs=[
            pl.BlockSpec(memory_space=pltpu.SMEM),
            pl.BlockSpec(memory_space=pltpu.VMEM),
        ],
        scratch_shapes=[pltpu.VMEM((3, ROWS, 128), f32)],
        compiler_params=params(),
        cost_estimate=cost(3e6, 6e6),
    )(place, start)


def blurred_columns(field, kx, out):
    for g in range(ZG):
        x = dot(kx[...].reshape(VIEWS * XR, EXR), field[g]).astype(bf16)
        out[:, g * XR : (g + 1) * XR, :] = x.reshape(VIEWS, XR, YE)


def blurred(x, ty, bz):
    y = dot(x, ty).astype(bf16)
    return [dot(bz, columns_of(y, XR, c)) for c in range(BX // GX)]


def columns_of(rows, stride, c):
    return jnp.concatenate(
        [rows[g * stride + c * GR : g * stride + (c + 1) * GR] for g in range(ZG)], axis=0
    )


def rows_from(groups):
    return jnp.concatenate(
        [part[g * GR : (g + 1) * GR] for g in range(ZG) for part in groups], axis=0
    )


def mirrored(quotient, kxt, tyt, bzt, out, first):
    y = dot(quotient, tyt).astype(bf16)
    x = [dot(kxt, y[g * XR : (g + 1) * XR]).astype(bf16) for g in range(ZG)]
    for c in range(EX // GX):
        rows = slice(c * GR, (c + 1) * GR)
        z = dot(bzt, jnp.concatenate([part[rows] for part in x], axis=0))
        for g in range(ZG):
            part = z[g * GR : (g + 1) * GR]
            out[g, rows, :] = part if first else out[g, rows, :] + part


def quotient_of(layer, code, blur_now):
    lane = iota(code.shape, 1)
    inside = (lane < YQ) | ((lane < TURN) & (layer < VIEWS - 1)) | ((lane >= TURN) & (layer > 0))
    measured = jnp.where(inside, from_code(code) * (1.0 / M_SCALE) + M_MID, 0.0)
    return (measured / jnp.where(inside, blur_now, 1.0)).astype(bf16)


def widened(own, from_left, from_right):
    inverse = 1.0 / E_SCALE
    return jnp.concatenate(
        [from_code(from_left) * inverse, own, from_code(from_right) * inverse], axis=1
    )


def blur_body(own, from_left, from_right, kx, ty, bz, out, field, columns):
    step = pl.program_id(0)

    @pl.when(step == 0)
    def _():
        field[...] = widened(own[...], from_left[...], from_right[...]).astype(bf16)
        blurred_columns(field, kx, columns)

    out[step] = rows_from(blurred(columns[step], ty[step], bz[step]))


def blur(own, from_left, from_right, mats):
    operands = kept([own, from_left, from_right, mats[0], mats[2], mats[4]])
    return pl.pallas_call(
        blur_body,
        grid=(VIEWS,),
        out_shape=pltpu.VMEM((VIEWS, ROWS, YE), f32),
        in_specs=[KEPT] * len(operands),
        out_specs=KEPT,
        scratch_shapes=[pltpu.VMEM((ZG, EXR, YE), bf16), pltpu.VMEM((VIEWS, ROWS, YE), bf16)],
        compiler_params=params(),
        cost_estimate=cost(7e9, 1.6e7),
    )(*operands)


def joined(parts):
    return jnp.concatenate([part[...] for part in parts], axis=0)


def grouped(refs, layout):
    refs = iter(refs)
    return [[next(refs) for _ in range(n)] for n in layout]


def mirror_body(views, layout, first, last, place, *rest):
    rest = list(rest)
    before = None if first else rest.pop(0)
    codes, rest = grouped(rest, layout), rest[sum(layout) :]
    blur_ref, kxt, tyt, bzt, total = rest[:5]
    if not first:
        total[...] = before[...]
    for r, parts in zip(views, codes):
        quotient = quotient_of(place[1], joined(parts), blur_ref[r])
        mirrored(quotient, kxt[r], tyt[r], bzt[r], total, first)
    if last:
        left, right = flat(total[:, : EXR // 2]), flat(total[:, EXR // 2 :])
        send_sides(send_wide, place, rest[5], rest[6], left, right, rest[7])


def mirror(place, before, codes, views, blur_all, mats, last):
    first = before is None
    layout = tuple(len(parts) for parts in codes)
    columns = jax.ShapeDtypeStruct((wide_rows(ZG * EXR // 2), YQ), i16)
    operands = [] if first else [before]
    operands += [part for parts in codes for part in parts]
    operands = kept(operands + [blur_all, mats[1], mats[3], mats[5]])
    return pl.pallas_call(
        functools.partial(mirror_body, views, layout, first, last),
        out_shape=(pltpu.VMEM((ZG, EXR, YE), f32),) + (columns,) * (2 * last),
        in_specs=[pl.BlockSpec(memory_space=pltpu.SMEM)] + [KEPT] * len(operands),
        out_specs=(KEPT,) * (1 + 2 * last),
        scratch_shapes=[pltpu.VMEM((2,) + columns.shape, i16)] * last,
        compiler_params=params(),
        cost_estimate=cost(2e9 * len(views), 8e6 * len(views)),
    )(place, *operands)


def second_body(layout, place, own, e_left, e_right, total, x_first, x_second, *rest):
    codes, rest = grouped(rest, layout), rest[sum(layout) :]
    kx, kxt, ty, tyt, bz, bzt = rest[:6]
    estimate, center, first, second, field, columns, acc, sides, held, sent = rest[6:]
    take_sides(place, x_first, x_second, sides)
    edge = MARGIN * ZI
    middle = EXR // 2
    start = widened(own[...], e_left[...], e_right[...]) * (1.0 / VIEWS)
    for half in range(2):
        came = sides.at[half]
        rows = slice(half * middle, (half + 1) * middle)
        now = start[:, rows] * (total[:, rows] + wide_value(came).reshape(ZG, middle, YE))
        field[:, rows] = now.astype(bf16)
        inner = now[:, edge:] if half == 0 else now[:, : middle - edge]
        estimate[:, half * edge : (half + 1) * edge] = inner[:, :, :YQ]
    blurred_columns(field, kx, columns)
    for r in range(VIEWS):
        held[r] = joined(codes[r])
    acc[...] = jnp.zeros_like(acc)

    def two_views(i, _):
        for r in (2 * i, 2 * i + 1):
            blur_now = rows_from(blurred(columns[r], ty[r], bz[r]))
            quotient = quotient_of(place[1], held[r], blur_now)
            mirrored(quotient, kxt[r], tyt[r, :, :YQ], bzt[r], acc, False)
        return 0

    lax.fori_loop(0, VIEWS // 2, two_views, 0)
    center[...] = acc[:, edge : edge + XR, :]
    left, right = flat(acc[:, :edge, :]), flat(acc[:, edge + XR :, :])
    send_sides(send, place, first, second, left, right, sent)


def second(place, own, e_left, e_right, total, x_first, x_second, codes, mats):
    columns = jax.ShapeDtypeStruct((ZG * MARGIN * ZI + 16, YQ), i16)
    cell_shape = pltpu.VMEM((ZG, XR, YQ), f32)
    layout = tuple(len(parts) for parts in codes)
    operands = [own, e_left, e_right, total, x_first, x_second]
    operands += [part for parts in codes for part in parts] + list(mats)
    operands = kept(operands)
    return pl.pallas_call(
        functools.partial(second_body, layout),
        out_shape=(cell_shape, cell_shape, columns, columns),
        in_specs=[pl.BlockSpec(memory_space=pltpu.SMEM)] + [KEPT] * len(operands),
        out_specs=(KEPT,) * 4,
        scratch_shapes=[
            pltpu.VMEM((ZG, EXR, YE), bf16),
            pltpu.VMEM((VIEWS, ROWS, YE), bf16),
            pltpu.VMEM((ZG, EXR, YQ), f32),
            pltpu.VMEM((2,) + x_first.shape, i16),
            pltpu.VMEM((VIEWS, ROWS, YE), i16),
            pltpu.VMEM((2,) + columns.shape, i16),
        ],
        compiler_params=params(),
        cost_estimate=cost(1.6e10, 4e7),
    )(place, *operands)


def finish_body(place, estimate, total, x_first, x_second, low, high, sides):
    take_sides(place, x_first, x_second, sides)
    middle = XR // 2
    a = total[:, :middle] + lane_value(sides.at[0]).reshape(ZG, middle, YQ)
    b = total[:, middle:] + lane_value(sides.at[1]).reshape(ZG, middle, YQ)
    send(low, flat(estimate[:, :middle] * a * (1.0 / VIEWS)))
    send(high, flat(estimate[:, middle:] * b * (1.0 / VIEWS)))


def finish(place, estimate, total, x_first, x_second):
    half = jax.ShapeDtypeStruct((ROWS // 2 + 16, YQ), i16)
    return pl.pallas_call(
        finish_body,
        out_shape=(half, half),
        in_specs=[pl.BlockSpec(memory_space=pltpu.SMEM)] + [KEPT] * 4,
        out_specs=(KEPT, KEPT),
        scratch_shapes=[pltpu.VMEM((2,) + x_first.shape, i16)],
        compiler_params=params(),
        cost_estimate=cost(5e6, 4e6),
    )(place, *kept([estimate, total, x_first, x_second]))


def spread_out(codes, scratch, store):
    middle = XR // 2
    for half in range(2):
        value = lane_value(codes[half])
        for c in range(2):
            scratch[half, c] = value[:, c * 128 : (c + 1) * 128]
            for z in range(NZ):
                rows = pl.ds(z // ZI * middle + z % ZI, BX // 2, stride=ZI)
                store(z, half, c, scratch[half, c, rows, :])


def gather_body(place, *rest):
    codes, out, scratch = rest[: 2 * VIEWS - 2], rest[2 * VIEWS - 2], rest[2 * VIEWS - 1]
    for i, r in enumerate((0, 1, 3)):
        at = lax.rem(place[1] + VIEWS - r, VIEWS) * YQ

        def store(z, half, c, value):
            lanes = pl.ds(pl.multiple_of(at + c * 128, 128), 128)
            out[z, half * BX // 2 : (half + 1) * BX // 2, lanes] = value

        spread_out(codes[2 * i : 2 * i + 2], scratch.at[i], store)


def gathered(place, codes):
    return pl.pallas_call(
        gather_body,
        out_shape=jax.ShapeDtypeStruct((NZ, BX, VIEWS * YQ), f32),
        in_specs=[pl.BlockSpec(memory_space=pltpu.SMEM)] + [KEPT] * len(codes),
        scratch_shapes=[pltpu.VMEM((VIEWS - 1, 2, 2, ROWS // 2, 128), f32)],
        compiler_params=params(),
        cost_estimate=cost(3e6, 6e6),
    )(place, *kept(codes))


def complete_body(place, low, high, _, out, scratch, quarter, sem):
    def store(z, half, c, value):
        quarter[z, half * BX // 2 : (half + 1) * BX // 2, c * 128 : (c + 1) * 128] = value

    spread_out((low, high), scratch, store)
    at = pl.multiple_of(lax.rem(place[1] + 2, VIEWS) * YQ, YQ)
    move = pltpu.make_async_copy(quarter, out.at[:, :, pl.ds(at, YQ)], sem)
    move.start()
    move.wait()


def completed(place, low, high, out):
    anywhere = pl.BlockSpec(memory_space=pl.ANY)
    vmem = pl.BlockSpec(memory_space=pltpu.VMEM)
    return pl.pallas_call(
        complete_body,
        out_shape=jax.ShapeDtypeStruct(out.shape, f32),
        in_specs=[pl.BlockSpec(memory_space=pltpu.SMEM), vmem, vmem, anywhere],
        out_specs=anywhere,
        input_output_aliases={3: 0},
        scratch_shapes=[
            pltpu.VMEM((2, 2, ROWS // 2, 128), f32),
            pltpu.VMEM((NZ, BX, YQ), f32),
            pltpu.SemaphoreType.DMA,
        ],
        compiler_params=params(),
        cost_estimate=cost(1e6, 2e6),
    )(place, *kept([low, high]), out)


def per_device(view_tiles, route_block, route_column, psf_taps, start_estimate):
    groups = lax.axis_size("block")
    cap = max(2, (2 * BX + groups - 1) // groups)
    me, layer = lax.axis_index("block"), lax.axis_index("view")
    place = jnp.stack([me, layer]).astype(i32)

    def around(x, shift):
        return lax.ppermute(x, "view", [(i, (i + shift) % VIEWS) for i in range(VIEWS)])

    def shifted(x, shift):
        pairs = [(i, i + shift) for i in range(groups) if 0 <= i + shift < groups]
        return lax.ppermute(x, "block", pairs)

    def swapped(x, start):
        pairs = []
        for i in range(start, groups - 1, 2):
            pairs += [(i, i + 1), (i + 1, i)]
        return lax.ppermute(x, "block", pairs) if pairs else jnp.zeros_like(x)

    outgoing = pack(cap, groups, route_block[0], route_column[0], view_tiles[0])
    arrived = lax.all_to_all(outgoing, "block", split_axis=0, concat_axis=0, tiled=True)

    psf, start_estimate, _ = lax.optimization_barrier((psf_taps[0], start_estimate, outgoing))
    kernel = psf / jnp.sum(psf, axis=1, keepdims=True)
    kernel = kernel.astype(bf16).astype(f32)
    taps = [kernel] + [around(kernel, r) for r in range(1, VIEWS)]
    own, to_left, to_right = cell(place, start_estimate)
    e_left, e_right = shifted(to_right, 1), shifted(to_left, -1)

    codes = unpack(cap, place, arrived)
    own, taps, codes = lax.optimization_barrier((own, taps, codes))
    low_on, high_on = around(codes[2], 1), around(codes[3], -1)
    codes = [
        [codes[0]],
        [around(codes[1], 1)],
        [around(low_on, 1), around(high_on, -1)],
        [around(codes[4], -1)],
    ]
    mats = bands(jnp.stack(taps).reshape(VIEWS, 3 * TAPS))
    blur_all = blur(own, e_left, e_right, mats)
    (total,) = mirror(place, None, codes[:1], [0], blur_all, mats, False)
    (total,) = mirror(place, total, [codes[1], codes[3]], [1, 3], blur_all, mats, False)
    total, first, second_part = mirror(place, total, codes[2:3], [2], blur_all, mats, True)
    x_first, x_second = swapped(first, 1), swapped(second_part, 0)
    estimate, center, first, second_part = second(
        place, own, e_left, e_right, total, x_first, x_second, codes, mats
    )
    x_first, x_second = swapped(first, 1), swapped(second_part, 0)
    low, high = finish(place, estimate, center, x_first, x_second)
    low_after, high_before = around(low, -1), around(high, 1)
    high_after, low_before = around(high, -1), around(low, 1)
    low_across, high_across = around(low_after, -1), around(high_before, 1)
    out = gathered(place, [low, high, low_before, high_before, low_after, high_after])
    return completed(place, low_across, high_across, out)


def solution(mesh):
    placed = (
        P("view", "block", None, None),
        P("view", "block"),
        P("view", "block"),
        P("view", None, None),
        P(None, "block", None),
    )
    return jax.shard_map(
        per_device, mesh=mesh, in_specs=placed, out_specs=P(None, "block", None), check_vma=False
    )
```

```python
import functools

import jax
import jax.numpy as jnp
import numpy as np
from jax import lax
from jax.experimental import pallas as pl
from jax.experimental.pallas import tpu as pltpu
from jax.sharding import PartitionSpec as P

ITERS = 2
TAPS = 31
HALF = 15
VIEWS = 4
NZ = 24
BX = 32
MARGIN = 16
EX = BX + 2 * MARGIN
YQ = 256
YE = 384
TURN = 320
ROWS = BX * NZ
ZI = 8
ZG = NZ // ZI
XR = BX * ZI
EXR = EX * ZI
GX = 8
GR = GX * ZI
ZR = GX * NZ
FULL = 32700.0
STEPS = 128.0
LN2 = float(np.log(2.0))
M_MID, M_SCALE = 2.125, 32767.0 / 1.875
E_SCALE = 32767.0 / 2.0
VMEM = 28 * 1024 * 1024

f32, bf16, i32, i16 = jnp.float32, jnp.bfloat16, jnp.int32, jnp.int16


def params(limit=VMEM):
    return pltpu.CompilerParams(vmem_limit_bytes=limit)


KEPT = pl.BlockSpec(memory_space=pltpu.VMEM)


def kept(operands):
    return [pltpu.with_memory_space_constraint(x, pltpu.VMEM) for x in operands]


def cost(flops, moved):
    return pl.CostEstimate(flops=int(flops), bytes_accessed=int(moved), transcendentals=0)


def dot(a, b):
    return jnp.dot(a, b, preferred_element_type=f32)


def to_code(x):
    return jnp.floor(x + 0.5).astype(i32).astype(i16)


def from_code(c):
    return c.astype(i32).astype(f32)


def scale_steps(top):
    return jnp.ceil(jnp.log(jnp.maximum(top, 1e-30)) * (STEPS / LN2))


def lane_code(value):
    k = scale_steps(jnp.max(jnp.abs(value), axis=0, keepdims=True))
    code = to_code(value * (jnp.exp(k * (-LN2 / STEPS)) * FULL))
    return code, jnp.broadcast_to(k, (16, value.shape[1])).astype(i32).astype(i16)


def lane_value(ref):
    n = ref.shape[0] - 16
    k = from_code(ref[n:])[0:1]
    return from_code(ref[:n]) * (jnp.exp(k * (LN2 / STEPS)) * (1.0 / FULL))


def send(ref, value):
    n = value.shape[0]
    ref[:n], ref[n:] = lane_code(value)


def margin_lanes(shape):
    lane = lax.broadcasted_iota(i32, shape, 1)
    return (lane < 32) | (lane >= 96)


def send_wide(ref, value):
    n = value.shape[0]
    k = scale_steps(jnp.max(jnp.abs(value), axis=0, keepdims=True))
    scaled = value * (jnp.exp(k * (-LN2 / STEPS)) * FULL)
    ref[:n] = to_code(scaled[:, :YQ])
    first, second = scaled[: n // 2, YQ:], scaled[n // 2 :, YQ:]
    shared = jnp.where(margin_lanes(first.shape), first, pltpu.roll(second, 64, 1))
    shared = jnp.concatenate([shared[: n // 4], shared[n // 4 :]], axis=1)
    ref[n : n + n // 4] = to_code(shared)
    k = jnp.concatenate([k[:, :YQ], k[:, YQ:], k[:, YQ:]], axis=1)
    k = jnp.broadcast_to(k, (16, 2 * YQ)).astype(i32).astype(i16)
    ref[n + n // 4 : n + n // 4 + 16] = k[:, :YQ]
    ref[n + n // 4 + 16 :] = k[:, YQ:]


def wide_rows(n):
    return n + n // 4 + 32


def wide_value(ref):
    n = (ref.shape[0] - 32) * 4 // 5
    at = n + n // 4
    center = from_code(ref[:n]) * (jnp.exp(from_code(ref[at : at + 16])[0:1] * (LN2 / STEPS)) / FULL)
    shared = from_code(ref[n:at])
    shared = jnp.concatenate([shared[:, :128], shared[:, 128:]], axis=0)
    ours = margin_lanes(shared.shape)
    first = jnp.where(ours, shared, 0.0)
    second = pltpu.roll(jnp.where(ours, 0.0, shared), 64, 1)
    k = from_code(ref[at + 16 :])[0:1, :128]
    ends = jnp.concatenate([first, second], axis=0) * (jnp.exp(k * (LN2 / STEPS)) / FULL)
    return jnp.concatenate([center, ends], axis=1)


def flat(x):
    return x.reshape(x.shape[0] * x.shape[1], x.shape[2])


def send_sides(encode, place, first, second, left, right, sides):
    encode(sides.at[0], left)
    encode(sides.at[1], right)
    even = lax.rem(place[0], 2) == 0

    @pl.when(even)
    def _():
        first[...], second[...] = sides[0], sides[1]

    @pl.when(jnp.logical_not(even))
    def _():
        first[...], second[...] = sides[1], sides[0]


def take_sides(place, first, second, sides):
    even = lax.rem(place[0], 2) == 0

    @pl.when(even)
    def _():
        sides[0], sides[1] = first[...], second[...]

    @pl.when(jnp.logical_not(even))
    def _():
        sides[0], sides[1] = second[...], first[...]


LOADS = 4
SLOT = NZ * 8


def pack_body(cap, blocks, columns, tiles, out, labels, count, slots, held, sent, loaded, pushed):
    pieces = tiles.shape[0]
    part = pieces // LOADS
    groups = out.shape[0]

    def load(i):
        rows = pl.ds(i * part, part)
        return pltpu.make_async_copy(tiles.at[rows], held.at[rows], loaded.at[i])

    for i in range(LOADS):
        load(i).start()

    def clear(i, _):
        labels[i] = 0
        return 0

    lax.fori_loop(0, groups * cap, clear, 0)

    def zero(i, _):
        count[i] = 0
        return 0

    lax.fori_loop(0, groups, zero, 0)

    def route(p, _):
        b = blocks[p]
        rank = count[b]
        count[b] = rank + 1
        slot = b * cap + rank
        labels[slot] = columns[p] + 1
        slots[p] = slot
        return 0

    lax.fori_loop(0, pieces, route, 0)
    lane = lax.broadcasted_iota(i32, (16, 128), 1)

    def mark(b, _):
        row = jnp.zeros((16, 128), i32)
        for rank in range(cap):
            row = jnp.where(lane == rank, labels[b * cap + rank], row)
        sent[b, cap * SLOT :, :] = row.astype(f32).astype(bf16)
        return 0

    lax.fori_loop(0, groups, mark, 0)
    def push(b, at, rows, sem):
        part = pl.ds(pl.multiple_of(at, 16), rows)
        return pltpu.make_async_copy(sent.at[b, part, :], out.at[b, part, :], sem)

    def tags():
        rows = pl.ds(cap * SLOT, 16)
        return pltpu.make_async_copy(sent.at[:, rows, :], out.at[:, rows, :], pushed.at[1])

    tags().start()
    for i in range(LOADS):
        load(i).wait()

        def put(p, _):
            slot = slots[p]
            b = slot // cap
            at = (slot - b * cap) * SLOT
            for c in range(8):
                rows = pl.ds(pl.multiple_of(at + 16 * c, 16), 16)
                sent[b, rows, :] = held[p, :16, 128 * c : 128 * (c + 1)]
            for c in range(0, 8, 2):
                rows = pl.ds(pl.multiple_of(at + 128 + 8 * c, 16), 16)
                sent[b, rows, :] = jnp.concatenate(
                    [
                        held[p, 16:, 128 * c : 128 * (c + 1)],
                        held[p, 16:, 128 * (c + 1) : 128 * (c + 2)],
                    ],
                    axis=0,
                )
            push(b, at, SLOT, pushed.at[0]).start()
            return 0

        lax.fori_loop(i * part, (i + 1) * part, put, 0, unroll=2)
    tags().wait()
    if pieces % cap == 0:
        every = pl.ds(0, pieces // cap), pl.ds(0, cap * SLOT)
        pltpu.make_async_copy(sent.at[every], out.at[every], pushed.at[0]).wait()
    else:
        lax.fori_loop(0, pieces, lambda p, _: push(0, 0, SLOT, pushed.at[0]).wait(), None)


def pack(cap, groups, blocks, columns, tiles):
    smem = pl.BlockSpec(memory_space=pltpu.SMEM)
    message = (groups, cap * SLOT + 16, 128)
    return pl.pallas_call(
        functools.partial(pack_body, cap),
        out_shape=pltpu.HBM(message, bf16),
        in_specs=[smem, smem, pl.BlockSpec(memory_space=pltpu.HBM)],
        out_specs=pl.BlockSpec(memory_space=pltpu.HBM),
        scratch_shapes=[
            pltpu.SMEM((groups * cap,), i32),
            pltpu.SMEM((groups,), i32),
            pltpu.SMEM((tiles.shape[0],), i32),
            pltpu.VMEM(tiles.shape, bf16),
            pltpu.VMEM(message, bf16),
            pltpu.SemaphoreType.DMA((LOADS,)),
            pltpu.SemaphoreType.DMA((2,)),
        ],
        compiler_params=params(2 * VMEM),
        cost_estimate=cost(0, 4 * tiles.size),
    )(blocks, columns, pltpu.with_memory_space_constraint(tiles, pltpu.HBM))


def tucked(code):
    n = code.shape[0]
    ends = from_code(code[:, YQ:])
    turned = [pltpu.roll(ends[j * n // 4 : (j + 1) * n // 4], 48, 1) for j in range(4)]
    lane = lax.broadcasted_iota(i32, turned[0].shape, 1)
    rows = [
        jnp.where(lane < 96, turned[i], pltpu.roll(turned[3], 96 - 32 * i, 1)) for i in range(3)
    ]
    rows = jnp.concatenate(rows, axis=0)
    half = 3 * n // 8
    rows = jnp.concatenate([rows[:half], rows[half:]], axis=1)
    return jnp.concatenate([code[:, :YQ], to_code(rows)], axis=0)


def untucked(part):
    if part.shape[1] == YE:
        return part[...]
    n = part.shape[0] * 8 // 11
    rows = from_code(part[n:])
    rows = jnp.concatenate([rows[:, :128], rows[:, 128:]], axis=0)
    rows = [rows[i * n // 4 : (i + 1) * n // 4] for i in range(3)]
    lane = lax.broadcasted_iota(i32, rows[0].shape, 1)
    last = pltpu.roll(rows[0], 32, 1)
    for i in (1, 2):
        moved = pltpu.roll(rows[i], 32 + 32 * i, 1)
        last = jnp.where((lane >= 32 * i) & (lane < 32 * i + 32), moved, last)
    ends = [pltpu.roll(row, 80, 1) for row in rows + [last]]
    return jnp.concatenate([part[:n], to_code(jnp.concatenate(ends, axis=0))], axis=1)


PART_VIEWS = (0, 1, 2, 2, 3)
PART_ROWS = (0, 0, 0, ROWS // 2, 0)


def unpack_body(cap, chunk, place, arrived, whole_arrived, *rest):
    outs, (acc, codes, count, marks, table, labels, sem) = rest[: VIEWS + 1], rest[VIEWS + 1 :]
    step = pl.program_id(0)
    layer = place[1]

    @pl.when(step == 0)
    def _():
        fetch = pltpu.make_async_copy(
            whole_arrived.at[:, pl.ds(cap * SLOT, 16), :], marks, sem.at[0]
        )
        fetch.start()
        acc[...] = jnp.zeros_like(acc)

        def zero(i, _):
            count[i] = 0
            return 0

        lax.fori_loop(0, BX, zero, 0)
        fetch.wait()
        ranks = table.shape[0]
        which = jnp.where(iota((ranks, 128), 0) == iota((ranks, 128), 1), 1.0, 0.0)
        lines = jnp.max(marks[...].astype(f32), axis=1)
        found = lax.dot_general(which, lines, (((1,), (1,)), ((), ())), preferred_element_type=f32)
        table[:, : lines.shape[0]] = found.astype(i32)
        move = pltpu.make_async_copy(table, labels, sem.at[1])
        move.start()
        move.wait()

    def from_source(j, _):
        for rank in range(cap):
            label = labels[rank, step * chunk + j]

            @pl.when(label > 0)
            def _():
                col = label - 1
                rows = pl.ds(pl.multiple_of(col * ZI, ZI), ZI)
                tile = arrived[j, rank * SLOT : (rank + 1) * SLOT, :].astype(f32)
                for c in range(8):
                    lanes = slice(128 * c, 128 * (c + 1))
                    acc[0, rows, lanes] += tile[16 * c : 16 * c + 8]
                    acc[1, rows, lanes] += tile[16 * c + 8 : 16 * c + 16]
                    acc[2, rows, lanes] += tile[128 + 8 * c : 136 + 8 * c]
                count[col] += 1

        return 0

    lax.fori_loop(0, chunk, from_source, 0, unroll=4)

    @pl.when(step == pl.num_programs(0) - 1)
    def _():
        row = lax.broadcasted_iota(i32, (2 * ZI, 128), 0)
        lane = lax.broadcasted_iota(i32, (2 * ZI, 128), 1)

        def pair(i, _):
            first = M_SCALE / jnp.maximum(count[2 * i], 1).astype(f32)
            second = M_SCALE / jnp.maximum(count[2 * i + 1], 1).astype(f32)
            inverse = jnp.where(row < ZI, first, second)
            for g in range(ZG):
                rows = pl.ds(pl.multiple_of(i * 2 * ZI, 2 * ZI), 2 * ZI)
                to = pl.ds(pl.multiple_of(g * XR + i * 2 * ZI, 2 * ZI), 2 * ZI)
                blocks = [
                    acc[g, rows, 128 * c : 128 * (c + 1)] * inverse - M_MID * M_SCALE
                    for c in range(2 * VIEWS)
                ]
                for v in range(VIEWS):
                    after = blocks[min(2 * v + 2, 2 * VIEWS - 1)]
                    before = blocks[max(2 * v - 1, 0)]
                    ends = jnp.where(lane < 64, after, before)
                    code = jnp.concatenate([blocks[2 * v], blocks[2 * v + 1], ends], axis=1)
                    codes[v, to, :] = to_code(code)
            return 0

        lax.fori_loop(0, BX // 2, pair, 0, unroll=2)
        for r, at, out in zip(PART_VIEWS, PART_ROWS, outs):
            n = out.shape[0] * 8 // 11 if r else out.shape[0]
            code = codes[lax.rem(layer + r, VIEWS), at : at + n, :]
            out[...] = tucked(code) if r else code


def unpack(cap, place, arrived):
    groups = arrived.shape[0]
    chunk = min(32, groups)
    rows = [ROWS // PART_VIEWS.count(r) for r in PART_VIEWS]
    shapes = [(n * 11 // 8, YQ) if r else (n, YE) for n, r in zip(rows, PART_VIEWS)]
    smem = pl.BlockSpec(memory_space=pltpu.SMEM)
    return pl.pallas_call(
        functools.partial(unpack_body, cap, chunk),
        grid=(groups // chunk,),
        out_shape=tuple(jax.ShapeDtypeStruct(shape, i16) for shape in shapes),
        in_specs=[
            smem,
            pl.BlockSpec((chunk,) + arrived.shape[1:], lambda s: (s, 0, 0)),
            pl.BlockSpec(memory_space=pl.ANY),
        ],
        out_specs=tuple(pl.BlockSpec(shape, lambda s: (0, 0)) for shape in shapes),
        scratch_shapes=[
            pltpu.VMEM((ZG, XR, VIEWS * YQ), f32),
            pltpu.VMEM((VIEWS, ROWS, YE), i16),
            pltpu.SMEM((BX,), i32),
            pltpu.VMEM((groups, 16, 128), bf16),
            pltpu.VMEM((max(8, cap), 128), i32),
            pltpu.SMEM((max(8, cap), 128), i32),
            pltpu.SemaphoreType.DMA((2,)),
        ],
        compiler_params=params(),
        cost_estimate=cost(arrived.size, 2 * arrived.size),
    )(place, arrived, arrived)


def iota(shape, dim):
    return lax.broadcasted_iota(i32, shape, dim)


def bands_body(taps, kx, kxt, ty, tyt, bz, bzt):
    r = pl.program_id(0)

    def band(distance, axis):
        out = jnp.zeros(distance.shape, f32)
        for t in range(TAPS):
            out = jnp.where(distance == t, taps[r, axis * TAPS + t], out)
        return out

    def circulant(row, n):
        wide = jnp.broadcast_to(row[0:1], (n, row.shape[1]))
        return pltpu.roll(wide, 0, 1, stride=1, stride_axis=0).astype(bf16)

    m = iota((8, EXR), 1)
    aligned = lax.bitwise_and(m, ZI - 1) == 0
    taps_at = band(lax.shift_right_logical(m, 3) - 1, 1)
    kx[r] = circulant(jnp.where(aligned, taps_at, 0.0), XR)
    taps_at = band(lax.shift_right_logical(EXR - m, 3) - 1, 1)
    kxt[r] = circulant(jnp.where(aligned, taps_at, 0.0), EXR)[:, :XR]
    n = iota((8, YE), 1)
    apart = jnp.where(n < YE // 2, n, n - YE)
    ty[r] = circulant(band(HALF - apart, 2), YE)
    back = circulant(band(HALF + apart, 2), YE)
    tyt[r] = back

    def parts(x):
        group = jnp.where(x >= 2 * GR, 2, jnp.where(x >= GR, 1, 0))
        within = x - group * GR
        return group * ZI + lax.bitwise_and(within, ZI - 1), lax.shift_right_logical(within, 3)

    (zr, xr), (zc, xc) = parts(iota((ZR, 1), 0)), parts(iota((1, ZR), 1))
    same = xr == xc
    bz[r] = jnp.where(same, band(zc - zr + HALF, 0), 0.0).astype(bf16)
    bzt[r] = jnp.where(same, band(zr - zc + HALF, 0), 0.0).astype(bf16)


MATS = [(XR, EXR), (EXR, XR), (YE, YE), (YE, YE), (ZR, ZR), (ZR, ZR)]


def bands(taps):
    return pl.pallas_call(
        bands_body,
        grid=(VIEWS,),
        out_shape=tuple(pltpu.VMEM((VIEWS,) + s, bf16) for s in MATS),
        in_specs=[pl.BlockSpec(memory_space=pltpu.SMEM)],
        out_specs=(KEPT,) * len(MATS),
        compiler_params=params(),
        cost_estimate=cost(4e9, 2e7),
    )(taps)


def cell_body(place, start, own, left, right, scratch):
    layer = place[1]
    last = start.shape[2] - 128
    after = jnp.minimum((layer + 1) * YQ, last)
    before = jnp.maximum(layer * YQ - 128, 0)
    lane = iota((BX, 128), 1)
    for z in range(NZ):
        rows = pl.ds(z // ZI * XR + z % ZI, BX, stride=ZI)
        for c in range(2):
            at = pl.multiple_of(layer * YQ + c * 128, 128)
            scratch[c, rows, :] = start[z, :, pl.ds(at, 128)]
        head = start[z, :, pl.ds(pl.multiple_of(after, 128), 128)]
        tail = start[z, :, pl.ds(pl.multiple_of(before, 128), 128)]
        head = jnp.where((lane < TURN - YQ) & (layer < VIEWS - 1), head, 0.0)
        tail = jnp.where((lane >= TURN - YQ) & (layer > 0), tail, 0.0)
        scratch[2, rows, :] = head + tail
    value = jnp.concatenate([scratch[c] for c in range(3)], axis=1)
    own[...] = value.reshape(ZG, XR, YE)
    code = to_code(value * E_SCALE).reshape(ZG, XR, YE)
    left[...] = code[:, : XR // 2]
    right[...] = code[:, XR // 2 :]


def cell(place, start):
    half = jax.ShapeDtypeStruct((ZG, XR // 2, YE), i16)
    return pl.pallas_call(
        cell_body,
        out_shape=(pltpu.VMEM((ZG, XR, YE), f32), half, half),
        in_specs=[
            pl.BlockSpec(memory_space=pltpu.SMEM),
            pl.BlockSpec(memory_space=pltpu.VMEM),
        ],
        scratch_shapes=[pltpu.VMEM((3, ROWS, 128), f32)],
        compiler_params=params(),
        cost_estimate=cost(3e6, 6e6),
    )(place, start)


def blurred_columns(field, kx, out):
    for g in range(ZG):
        x = dot(kx[...].reshape(VIEWS * XR, EXR), field[g]).astype(bf16)
        out[:, g * XR : (g + 1) * XR, :] = x.reshape(VIEWS, XR, YE)


def blurred(x, ty, bz):
    y = dot(x, ty).astype(bf16)
    return [dot(bz, columns_of(y, XR, c)) for c in range(BX // GX)]


def columns_of(rows, stride, c):
    return jnp.concatenate(
        [rows[g * stride + c * GR : g * stride + (c + 1) * GR] for g in range(ZG)], axis=0
    )


def rows_from(groups):
    return jnp.concatenate(
        [part[g * GR : (g + 1) * GR] for g in range(ZG) for part in groups], axis=0
    )


def mirrored(quotient, kxt, tyt, bzt, out, first):
    y = dot(quotient, tyt).astype(bf16)
    x = [dot(kxt, y[g * XR : (g + 1) * XR]).astype(bf16) for g in range(ZG)]
    for c in range(EX // GX):
        rows = slice(c * GR, (c + 1) * GR)
        z = dot(bzt, jnp.concatenate([part[rows] for part in x], axis=0))
        for g in range(ZG):
            part = z[g * GR : (g + 1) * GR]
            out[g, rows, :] = part if first else out[g, rows, :] + part


def quotient_of(layer, code, blur_now):
    lane = iota(code.shape, 1)
    inside = (lane < YQ) | ((lane < TURN) & (layer < VIEWS - 1)) | ((lane >= TURN) & (layer > 0))
    measured = jnp.where(inside, from_code(code) * (1.0 / M_SCALE) + M_MID, 0.0)
    return (measured / jnp.where(inside, blur_now, 1.0)).astype(bf16)


def widened(own, from_left, from_right):
    inverse = 1.0 / E_SCALE
    return jnp.concatenate(
        [from_code(from_left) * inverse, own, from_code(from_right) * inverse], axis=1
    )


def blur_body(own, from_left, from_right, kx, ty, bz, out, field, columns):
    step = pl.program_id(0)

    @pl.when(step == 0)
    def _():
        field[...] = widened(own[...], from_left[...], from_right[...]).astype(bf16)
        blurred_columns(field, kx, columns)

    out[step] = rows_from(blurred(columns[step], ty[step], bz[step]))


def blur(own, from_left, from_right, mats):
    operands = kept([own, from_left, from_right, mats[0], mats[2], mats[4]])
    return pl.pallas_call(
        blur_body,
        grid=(VIEWS,),
        out_shape=pltpu.VMEM((VIEWS, ROWS, YE), f32),
        in_specs=[KEPT] * len(operands),
        out_specs=KEPT,
        scratch_shapes=[pltpu.VMEM((ZG, EXR, YE), bf16), pltpu.VMEM((VIEWS, ROWS, YE), bf16)],
        compiler_params=params(),
        cost_estimate=cost(7e9, 1.6e7),
    )(*operands)


def joined(parts):
    return jnp.concatenate([untucked(part) for part in parts], axis=0)


def grouped(refs, layout):
    refs = iter(refs)
    return [[next(refs) for _ in range(n)] for n in layout]


def mirror_body(views, layout, first, last, place, *rest):
    rest = list(rest)
    before = None if first else rest.pop(0)
    codes, rest = grouped(rest, layout), rest[sum(layout) :]
    blur_ref, kxt, tyt, bzt, total = rest[:5]
    if not first:
        total[...] = before[...]
    for r, parts in zip(views, codes):
        quotient = quotient_of(place[1], joined(parts), blur_ref[r])
        mirrored(quotient, kxt[r], tyt[r], bzt[r], total, first)
    if last:
        left, right = flat(total[:, : EXR // 2]), flat(total[:, EXR // 2 :])
        send_sides(send_wide, place, rest[5], rest[6], left, right, rest[7])


def mirror(place, before, codes, views, blur_all, mats, last):
    first = before is None
    layout = tuple(len(parts) for parts in codes)
    columns = jax.ShapeDtypeStruct((wide_rows(ZG * EXR // 2), YQ), i16)
    operands = [] if first else [before]
    operands += [part for parts in codes for part in parts]
    operands = kept(operands + [blur_all, mats[1], mats[3], mats[5]])
    return pl.pallas_call(
        functools.partial(mirror_body, views, layout, first, last),
        out_shape=(pltpu.VMEM((ZG, EXR, YE), f32),) + (columns,) * (2 * last),
        in_specs=[pl.BlockSpec(memory_space=pltpu.SMEM)] + [KEPT] * len(operands),
        out_specs=(KEPT,) * (1 + 2 * last),
        scratch_shapes=[pltpu.VMEM((2,) + columns.shape, i16)] * last,
        compiler_params=params(),
        cost_estimate=cost(2e9 * len(views), 8e6 * len(views)),
    )(place, *operands)


def second_body(layout, place, own, e_left, e_right, total, x_first, x_second, *rest):
    codes, rest = grouped(rest, layout), rest[sum(layout) :]
    kx, kxt, ty, tyt, bz, bzt = rest[:6]
    estimate, center, first, second, field, columns, acc, sides, held, sent = rest[6:]
    take_sides(place, x_first, x_second, sides)
    edge = MARGIN * ZI
    middle = EXR // 2
    start = widened(own[...], e_left[...], e_right[...]) * (1.0 / VIEWS)
    for half in range(2):
        came = sides.at[half]
        rows = slice(half * middle, (half + 1) * middle)
        now = start[:, rows] * (total[:, rows] + wide_value(came).reshape(ZG, middle, YE))
        field[:, rows] = now.astype(bf16)
        inner = now[:, edge:] if half == 0 else now[:, : middle - edge]
        estimate[:, half * edge : (half + 1) * edge] = inner[:, :, :YQ]
    blurred_columns(field, kx, columns)
    for r in range(VIEWS):
        held[r] = joined(codes[r])
    acc[...] = jnp.zeros_like(acc)

    def two_views(i, _):
        for r in (2 * i, 2 * i + 1):
            blur_now = rows_from(blurred(columns[r], ty[r], bz[r]))
            quotient = quotient_of(place[1], held[r], blur_now)
            mirrored(quotient, kxt[r], tyt[r, :, :YQ], bzt[r], acc, False)
        return 0

    lax.fori_loop(0, VIEWS // 2, two_views, 0)
    center[...] = acc[:, edge : edge + XR, :]
    left, right = flat(acc[:, :edge, :]), flat(acc[:, edge + XR :, :])
    send_sides(send, place, first, second, left, right, sent)


def second(place, own, e_left, e_right, total, x_first, x_second, codes, mats):
    columns = jax.ShapeDtypeStruct((ZG * MARGIN * ZI + 16, YQ), i16)
    cell_shape = pltpu.VMEM((ZG, XR, YQ), f32)
    layout = tuple(len(parts) for parts in codes)
    operands = [own, e_left, e_right, total, x_first, x_second]
    operands += [part for parts in codes for part in parts] + list(mats)
    operands = kept(operands)
    return pl.pallas_call(
        functools.partial(second_body, layout),
        out_shape=(cell_shape, cell_shape, columns, columns),
        in_specs=[pl.BlockSpec(memory_space=pltpu.SMEM)] + [KEPT] * len(operands),
        out_specs=(KEPT,) * 4,
        scratch_shapes=[
            pltpu.VMEM((ZG, EXR, YE), bf16),
            pltpu.VMEM((VIEWS, ROWS, YE), bf16),
            pltpu.VMEM((ZG, EXR, YQ), f32),
            pltpu.VMEM((2,) + x_first.shape, i16),
            pltpu.VMEM((VIEWS, ROWS, YE), i16),
            pltpu.VMEM((2,) + columns.shape, i16),
        ],
        compiler_params=params(),
        cost_estimate=cost(1.6e10, 4e7),
    )(place, *operands)


def finish_body(place, estimate, total, x_first, x_second, low, high, sides):
    take_sides(place, x_first, x_second, sides)
    middle = XR // 2
    a = total[:, :middle] + lane_value(sides.at[0]).reshape(ZG, middle, YQ)
    b = total[:, middle:] + lane_value(sides.at[1]).reshape(ZG, middle, YQ)
    send(low, flat(estimate[:, :middle] * a * (1.0 / VIEWS)))
    send(high, flat(estimate[:, middle:] * b * (1.0 / VIEWS)))


def finish(place, estimate, total, x_first, x_second):
    half = jax.ShapeDtypeStruct((ROWS // 2 + 16, YQ), i16)
    return pl.pallas_call(
        finish_body,
        out_shape=(half, half),
        in_specs=[pl.BlockSpec(memory_space=pltpu.SMEM)] + [KEPT] * 4,
        out_specs=(KEPT, KEPT),
        scratch_shapes=[pltpu.VMEM((2,) + x_first.shape, i16)],
        compiler_params=params(),
        cost_estimate=cost(5e6, 4e6),
    )(place, *kept([estimate, total, x_first, x_second]))


def spread_out(codes, scratch, store):
    middle = XR // 2
    for half in range(2):
        value = lane_value(codes[half])
        for c in range(2):
            scratch[half, c] = value[:, c * 128 : (c + 1) * 128]
            for z in range(NZ):
                rows = pl.ds(z // ZI * middle + z % ZI, BX // 2, stride=ZI)
                store(z, half, c, scratch[half, c, rows, :])


def gather_body(place, *rest):
    codes, out, scratch = rest[: 2 * VIEWS - 2], rest[2 * VIEWS - 2], rest[2 * VIEWS - 1]
    for i, r in enumerate((0, 1, 3)):
        at = lax.rem(place[1] + VIEWS - r, VIEWS) * YQ

        def store(z, half, c, value):
            lanes = pl.ds(pl.multiple_of(at + c * 128, 128), 128)
            out[z, half * BX // 2 : (half + 1) * BX // 2, lanes] = value

        spread_out(codes[2 * i : 2 * i + 2], scratch.at[i], store)


def gathered(place, codes):
    return pl.pallas_call(
        gather_body,
        out_shape=jax.ShapeDtypeStruct((NZ, BX, VIEWS * YQ), f32),
        in_specs=[pl.BlockSpec(memory_space=pltpu.SMEM)] + [KEPT] * len(codes),
        scratch_shapes=[pltpu.VMEM((VIEWS - 1, 2, 2, ROWS // 2, 128), f32)],
        compiler_params=params(),
        cost_estimate=cost(3e6, 6e6),
    )(place, *kept(codes))


def complete_body(place, low, high, _, out, scratch, quarter, sem):
    def store(z, half, c, value):
        quarter[z, half * BX // 2 : (half + 1) * BX // 2, c * 128 : (c + 1) * 128] = value

    spread_out((low, high), scratch, store)
    at = pl.multiple_of(lax.rem(place[1] + 2, VIEWS) * YQ, YQ)
    move = pltpu.make_async_copy(quarter, out.at[:, :, pl.ds(at, YQ)], sem)
    move.start()
    move.wait()


def completed(place, low, high, out):
    anywhere = pl.BlockSpec(memory_space=pl.ANY)
    vmem = pl.BlockSpec(memory_space=pltpu.VMEM)
    return pl.pallas_call(
        complete_body,
        out_shape=jax.ShapeDtypeStruct(out.shape, f32),
        in_specs=[pl.BlockSpec(memory_space=pltpu.SMEM), vmem, vmem, anywhere],
        out_specs=anywhere,
        input_output_aliases={3: 0},
        scratch_shapes=[
            pltpu.VMEM((2, 2, ROWS // 2, 128), f32),
            pltpu.VMEM((NZ, BX, YQ), f32),
            pltpu.SemaphoreType.DMA,
        ],
        compiler_params=params(),
        cost_estimate=cost(1e6, 2e6),
    )(place, *kept([low, high]), out)


def per_device(view_tiles, route_block, route_column, psf_taps, start_estimate):
    groups = lax.axis_size("block")
    cap = max(2, (2 * BX + groups - 1) // groups)
    me, layer = lax.axis_index("block"), lax.axis_index("view")
    place = jnp.stack([me, layer]).astype(i32)

    def around(x, shift):
        return lax.ppermute(x, "view", [(i, (i + shift) % VIEWS) for i in range(VIEWS)])

    def shifted(x, shift):
        pairs = [(i, i + shift) for i in range(groups) if 0 <= i + shift < groups]
        return lax.ppermute(x, "block", pairs)

    def swapped(x, start):
        pairs = []
        for i in range(start, groups - 1, 2):
            pairs += [(i, i + 1), (i + 1, i)]
        return lax.ppermute(x, "block", pairs) if pairs else jnp.zeros_like(x)

    outgoing = pack(cap, groups, route_block[0], route_column[0], view_tiles[0])
    arrived = lax.all_to_all(outgoing, "block", split_axis=0, concat_axis=0, tiled=True)

    psf, start_estimate, _ = lax.optimization_barrier((psf_taps[0], start_estimate, outgoing))
    kernel = psf / jnp.sum(psf, axis=1, keepdims=True)
    kernel = kernel.astype(bf16).astype(f32)
    taps = [kernel] + [around(kernel, r) for r in range(1, VIEWS)]
    own, to_left, to_right = cell(place, start_estimate)
    e_left, e_right = shifted(to_right, 1), shifted(to_left, -1)

    codes = unpack(cap, place, arrived)
    own, taps, codes = lax.optimization_barrier((own, taps, codes))
    low_on, high_on = around(codes[2], 1), around(codes[3], -1)
    codes = [
        [codes[0]],
        [around(codes[1], 1)],
        [around(low_on, 1), around(high_on, -1)],
        [around(codes[4], -1)],
    ]
    mats = bands(jnp.stack(taps).reshape(VIEWS, 3 * TAPS))
    blur_all = blur(own, e_left, e_right, mats)
    (total,) = mirror(place, None, codes[:1], [0], blur_all, mats, False)
    (total,) = mirror(place, total, [codes[1], codes[3]], [1, 3], blur_all, mats, False)
    total, first, second_part = mirror(place, total, codes[2:3], [2], blur_all, mats, True)
    x_first, x_second = swapped(first, 1), swapped(second_part, 0)
    estimate, center, first, second_part = second(
        place, own, e_left, e_right, total, x_first, x_second, codes, mats
    )
    x_first, x_second = swapped(first, 1), swapped(second_part, 0)
    low, high = finish(place, estimate, center, x_first, x_second)
    low_after, high_before = around(low, -1), around(high, 1)
    high_after, low_before = around(high, -1), around(low, 1)
    low_across, high_across = around(low_after, -1), around(high_before, 1)
    out = gathered(place, [low, high, low_before, high_before, low_after, high_after])
    return completed(place, low_across, high_across, out)


def solution(mesh):
    placed = (
        P("view", "block", None, None),
        P("view", "block"),
        P("view", "block"),
        P("view", None, None),
        P(None, "block", None),
    )
    return jax.shard_map(
        per_device, mesh=mesh, in_specs=placed, out_specs=P(None, "block", None), check_vma=False
    )
```

```python
import functools

import jax
import jax.numpy as jnp
import numpy as np
from jax import lax
from jax.experimental import pallas as pl
from jax.experimental.pallas import tpu as pltpu
from jax.sharding import PartitionSpec as P

ITERS = 2
TAPS = 31
HALF = 15
VIEWS = 4
NZ = 24
BX = 32
MARGIN = 16
EX = BX + 2 * MARGIN
YQ = 256
YE = 384
TURN = 320
ROWS = BX * NZ
ZI = 8
ZG = NZ // ZI
XR = BX * ZI
EXR = EX * ZI
GX = 8
GR = GX * ZI
ZR = GX * NZ
FULL = 32700.0
STEPS = 128.0
LN2 = float(np.log(2.0))
M_MID, M_SCALE = 2.125, 32767.0 / 1.875
E_SCALE = 32767.0 / 2.0
VMEM = 28 * 1024 * 1024

f32, bf16, i32, i16 = jnp.float32, jnp.bfloat16, jnp.int32, jnp.int16


def params(limit=VMEM):
    return pltpu.CompilerParams(vmem_limit_bytes=limit)


KEPT = pl.BlockSpec(memory_space=pltpu.VMEM)


def kept(operands):
    return [pltpu.with_memory_space_constraint(x, pltpu.VMEM) for x in operands]


def cost(flops, moved):
    return pl.CostEstimate(flops=int(flops), bytes_accessed=int(moved), transcendentals=0)


def dot(a, b):
    return jnp.dot(a, b, preferred_element_type=f32)


def to_code(x):
    return jnp.floor(x + 0.5).astype(i32).astype(i16)


def from_code(c):
    return c.astype(i32).astype(f32)


def scale_steps(top):
    return jnp.ceil(jnp.log(jnp.maximum(top, 1e-30)) * (STEPS / LN2))


def lane_code(value):
    k = scale_steps(jnp.max(jnp.abs(value), axis=0, keepdims=True))
    code = to_code(value * (jnp.exp(k * (-LN2 / STEPS)) * FULL))
    return code, jnp.broadcast_to(k, (16, value.shape[1])).astype(i32).astype(i16)


def lane_value(ref):
    n = ref.shape[0] - 16
    k = from_code(ref[n:])[0:1]
    return from_code(ref[:n]) * (jnp.exp(k * (LN2 / STEPS)) * (1.0 / FULL))


def send(ref, value):
    n = value.shape[0]
    ref[:n], ref[n:] = lane_code(value)


def margin_lanes(shape):
    lane = lax.broadcasted_iota(i32, shape, 1)
    return (lane < 32) | (lane >= 96)


def send_wide(ref, value):
    n = value.shape[0]
    k = scale_steps(jnp.max(jnp.abs(value), axis=0, keepdims=True))
    scaled = value * (jnp.exp(k * (-LN2 / STEPS)) * FULL)
    ref[:n] = to_code(scaled[:, :YQ])
    first, second = scaled[: n // 2, YQ:], scaled[n // 2 :, YQ:]
    shared = jnp.where(margin_lanes(first.shape), first, pltpu.roll(second, 64, 1))
    shared = jnp.concatenate([shared[: n // 4], shared[n // 4 :]], axis=1)
    ref[n : n + n // 4] = to_code(shared)
    k = jnp.concatenate([k[:, :YQ], k[:, YQ:], k[:, YQ:]], axis=1)
    k = jnp.broadcast_to(k, (16, 2 * YQ)).astype(i32).astype(i16)
    ref[n + n // 4 : n + n // 4 + 16] = k[:, :YQ]
    ref[n + n // 4 + 16 :] = k[:, YQ:]


def wide_rows(n):
    return n + n // 4 + 32


def wide_value(ref):
    n = (ref.shape[0] - 32) * 4 // 5
    at = n + n // 4
    center = from_code(ref[:n]) * (jnp.exp(from_code(ref[at : at + 16])[0:1] * (LN2 / STEPS)) / FULL)
    shared = from_code(ref[n:at])
    shared = jnp.concatenate([shared[:, :128], shared[:, 128:]], axis=0)
    ours = margin_lanes(shared.shape)
    first = jnp.where(ours, shared, 0.0)
    second = pltpu.roll(jnp.where(ours, 0.0, shared), 64, 1)
    k = from_code(ref[at + 16 :])[0:1, :128]
    ends = jnp.concatenate([first, second], axis=0) * (jnp.exp(k * (LN2 / STEPS)) / FULL)
    return jnp.concatenate([center, ends], axis=1)


def flat(x):
    return x.reshape(x.shape[0] * x.shape[1], x.shape[2])


def send_sides(encode, place, first, second, left, right, sides):
    encode(sides.at[0], left)
    encode(sides.at[1], right)
    even = lax.rem(place[0], 2) == 0

    @pl.when(even)
    def _():
        first[...], second[...] = sides[0], sides[1]

    @pl.when(jnp.logical_not(even))
    def _():
        first[...], second[...] = sides[1], sides[0]


def take_sides(place, first, second, sides):
    even = lax.rem(place[0], 2) == 0

    @pl.when(even)
    def _():
        sides[0], sides[1] = first[...], second[...]

    @pl.when(jnp.logical_not(even))
    def _():
        sides[0], sides[1] = second[...], first[...]


LOADS = 4
SLOT = NZ * 8


def pack_body(cap, blocks, columns, tiles, out, labels, count, slots, held, sent, loaded, pushed):
    pieces = tiles.shape[0]
    part = pieces // LOADS
    groups = out.shape[0]

    def load(i):
        rows = pl.ds(i * part, part)
        return pltpu.make_async_copy(tiles.at[rows], held.at[rows], loaded.at[i])

    for i in range(LOADS):
        load(i).start()

    def clear(i, _):
        labels[i] = 0
        return 0

    lax.fori_loop(0, groups * cap, clear, 0)

    def zero(i, _):
        count[i] = 0
        return 0

    lax.fori_loop(0, groups, zero, 0)

    def route(p, _):
        b = blocks[p]
        rank = count[b]
        count[b] = rank + 1
        slot = b * cap + rank
        labels[slot] = columns[p] + 1
        slots[p] = slot
        return 0

    lax.fori_loop(0, pieces, route, 0, unroll=2)
    lane = lax.broadcasted_iota(i32, (16, 128), 1)

    def mark(b, _):
        row = jnp.zeros((16, 128), i32)
        for rank in range(cap):
            row = jnp.where(lane == rank, labels[b * cap + rank], row)
        sent[b, cap * SLOT :, :] = row.astype(f32).astype(bf16)
        return 0

    lax.fori_loop(0, groups, mark, 0, unroll=2)
    def push(b, at, rows, sem):
        part = pl.ds(pl.multiple_of(at, 16), rows)
        return pltpu.make_async_copy(sent.at[b, part, :], out.at[b, part, :], sem)

    def tags():
        rows = pl.ds(cap * SLOT, 16)
        return pltpu.make_async_copy(sent.at[:, rows, :], out.at[:, rows, :], pushed.at[1])

    tags().start()
    for i in range(LOADS):
        load(i).wait()

        def put(p, _):
            slot = slots[p]
            b = slot // cap
            at = (slot - b * cap) * SLOT
            for c in range(8):
                rows = pl.ds(pl.multiple_of(at + 16 * c, 16), 16)
                sent[b, rows, :] = held[p, :16, 128 * c : 128 * (c + 1)]
            for c in range(0, 8, 2):
                rows = pl.ds(pl.multiple_of(at + 128 + 8 * c, 16), 16)
                sent[b, rows, :] = jnp.concatenate(
                    [
                        held[p, 16:, 128 * c : 128 * (c + 1)],
                        held[p, 16:, 128 * (c + 1) : 128 * (c + 2)],
                    ],
                    axis=0,
                )
            push(b, at, SLOT, pushed.at[0]).start()
            return 0

        lax.fori_loop(i * part, (i + 1) * part, put, 0, unroll=2)
    tags().wait()
    if pieces % cap == 0:
        every = pl.ds(0, pieces // cap), pl.ds(0, cap * SLOT)
        pltpu.make_async_copy(sent.at[every], out.at[every], pushed.at[0]).wait()
    else:
        lax.fori_loop(0, pieces, lambda p, _: push(0, 0, SLOT, pushed.at[0]).wait(), None)


def pack(cap, groups, blocks, columns, tiles):
    smem = pl.BlockSpec(memory_space=pltpu.SMEM)
    message = (groups, cap * SLOT + 16, 128)
    return pl.pallas_call(
        functools.partial(pack_body, cap),
        out_shape=pltpu.HBM(message, bf16),
        in_specs=[smem, smem, pl.BlockSpec(memory_space=pltpu.HBM)],
        out_specs=pl.BlockSpec(memory_space=pltpu.HBM),
        scratch_shapes=[
            pltpu.SMEM((groups * cap,), i32),
            pltpu.SMEM((groups,), i32),
            pltpu.SMEM((tiles.shape[0],), i32),
            pltpu.VMEM(tiles.shape, bf16),
            pltpu.VMEM(message, bf16),
            pltpu.SemaphoreType.DMA((LOADS,)),
            pltpu.SemaphoreType.DMA((2,)),
        ],
        compiler_params=params(2 * VMEM),
        cost_estimate=cost(0, 4 * tiles.size),
    )(blocks, columns, pltpu.with_memory_space_constraint(tiles, pltpu.HBM))


def tucked(code):
    n = code.shape[0]
    ends = from_code(code[:, YQ:])
    turned = [pltpu.roll(ends[j * n // 4 : (j + 1) * n // 4], 48, 1) for j in range(4)]
    lane = lax.broadcasted_iota(i32, turned[0].shape, 1)
    rows = [
        jnp.where(lane < 96, turned[i], pltpu.roll(turned[3], 96 - 32 * i, 1)) for i in range(3)
    ]
    rows = jnp.concatenate(rows, axis=0)
    half = 3 * n // 8
    rows = jnp.concatenate([rows[:half], rows[half:]], axis=1)
    return jnp.concatenate([code[:, :YQ], to_code(rows)], axis=0)


def untucked(part):
    if part.shape[1] == YE:
        return part[...]
    n = part.shape[0] * 8 // 11
    rows = from_code(part[n:])
    rows = jnp.concatenate([rows[:, :128], rows[:, 128:]], axis=0)
    rows = [rows[i * n // 4 : (i + 1) * n // 4] for i in range(3)]
    lane = lax.broadcasted_iota(i32, rows[0].shape, 1)
    last = pltpu.roll(rows[0], 32, 1)
    for i in (1, 2):
        moved = pltpu.roll(rows[i], 32 + 32 * i, 1)
        last = jnp.where((lane >= 32 * i) & (lane < 32 * i + 32), moved, last)
    ends = [pltpu.roll(row, 80, 1) for row in rows + [last]]
    return jnp.concatenate([part[:n], to_code(jnp.concatenate(ends, axis=0))], axis=1)


PART_VIEWS = (0, 1, 2, 2, 3)
PART_ROWS = (0, 0, 0, ROWS // 2, 0)


def unpack_body(cap, chunk, place, arrived, whole_arrived, *rest):
    outs, (acc, codes, count, marks, table, labels, sem) = rest[: VIEWS + 1], rest[VIEWS + 1 :]
    step = pl.program_id(0)
    layer = place[1]

    @pl.when(step == 0)
    def _():
        fetch = pltpu.make_async_copy(
            whole_arrived.at[:, pl.ds(cap * SLOT, 16), :], marks, sem.at[0]
        )
        fetch.start()
        acc[...] = jnp.zeros_like(acc)

        def zero(i, _):
            count[i] = 0
            return 0

        lax.fori_loop(0, BX, zero, 0)
        fetch.wait()
        ranks = table.shape[0]
        which = jnp.where(iota((ranks, 128), 0) == iota((ranks, 128), 1), 1.0, 0.0)
        lines = jnp.max(marks[...].astype(f32), axis=1)
        found = lax.dot_general(which, lines, (((1,), (1,)), ((), ())), preferred_element_type=f32)
        table[:, : lines.shape[0]] = found.astype(i32)
        move = pltpu.make_async_copy(table, labels, sem.at[1])
        move.start()
        move.wait()

    def from_source(j, _):
        for rank in range(cap):
            label = labels[rank, step * chunk + j]

            @pl.when(label > 0)
            def _():
                col = label - 1
                rows = pl.ds(pl.multiple_of(col * ZI, ZI), ZI)
                tile = arrived[j, rank * SLOT : (rank + 1) * SLOT, :].astype(f32)
                for c in range(8):
                    lanes = slice(128 * c, 128 * (c + 1))
                    acc[0, rows, lanes] += tile[16 * c : 16 * c + 8]
                    acc[1, rows, lanes] += tile[16 * c + 8 : 16 * c + 16]
                    acc[2, rows, lanes] += tile[128 + 8 * c : 136 + 8 * c]
                count[col] += 1

        return 0

    lax.fori_loop(0, chunk, from_source, 0, unroll=8)

    @pl.when(step == pl.num_programs(0) - 1)
    def _():
        row = lax.broadcasted_iota(i32, (2 * ZI, 128), 0)
        lane = lax.broadcasted_iota(i32, (2 * ZI, 128), 1)

        def pair(i, _):
            first = M_SCALE / jnp.maximum(count[2 * i], 1).astype(f32)
            second = M_SCALE / jnp.maximum(count[2 * i + 1], 1).astype(f32)
            inverse = jnp.where(row < ZI, first, second)
            for g in range(ZG):
                rows = pl.ds(pl.multiple_of(i * 2 * ZI, 2 * ZI), 2 * ZI)
                to = pl.ds(pl.multiple_of(g * XR + i * 2 * ZI, 2 * ZI), 2 * ZI)
                blocks = [
                    acc[g, rows, 128 * c : 128 * (c + 1)] * inverse - M_MID * M_SCALE
                    for c in range(2 * VIEWS)
                ]
                for v in range(VIEWS):
                    after = blocks[min(2 * v + 2, 2 * VIEWS - 1)]
                    before = blocks[max(2 * v - 1, 0)]
                    ends = jnp.where(lane < 64, after, before)
                    code = jnp.concatenate([blocks[2 * v], blocks[2 * v + 1], ends], axis=1)
                    codes[v, to, :] = to_code(code)
            return 0

        lax.fori_loop(0, BX // 2, pair, 0, unroll=4)
        for r, at, out in zip(PART_VIEWS, PART_ROWS, outs):
            n = out.shape[0] * 8 // 11 if r else out.shape[0]
            code = codes[lax.rem(layer + r, VIEWS), at : at + n, :]
            out[...] = tucked(code) if r else code


def unpack(cap, place, arrived):
    groups = arrived.shape[0]
    chunk = min(32, groups)
    rows = [ROWS // PART_VIEWS.count(r) for r in PART_VIEWS]
    shapes = [(n * 11 // 8, YQ) if r else (n, YE) for n, r in zip(rows, PART_VIEWS)]
    smem = pl.BlockSpec(memory_space=pltpu.SMEM)
    return pl.pallas_call(
        functools.partial(unpack_body, cap, chunk),
        grid=(groups // chunk,),
        out_shape=tuple(jax.ShapeDtypeStruct(shape, i16) for shape in shapes),
        in_specs=[
            smem,
            pl.BlockSpec((chunk,) + arrived.shape[1:], lambda s: (s, 0, 0)),
            pl.BlockSpec(memory_space=pl.ANY),
        ],
        out_specs=tuple(pl.BlockSpec(shape, lambda s: (0, 0)) for shape in shapes),
        scratch_shapes=[
            pltpu.VMEM((ZG, XR, VIEWS * YQ), f32),
            pltpu.VMEM((VIEWS, ROWS, YE), i16),
            pltpu.SMEM((BX,), i32),
            pltpu.VMEM((groups, 16, 128), bf16),
            pltpu.VMEM((max(8, cap), 128), i32),
            pltpu.SMEM((max(8, cap), 128), i32),
            pltpu.SemaphoreType.DMA((2,)),
        ],
        compiler_params=params(),
        cost_estimate=cost(arrived.size, 2 * arrived.size),
    )(place, arrived, arrived)


def iota(shape, dim):
    return lax.broadcasted_iota(i32, shape, dim)


def bands_body(taps, kx, kxt, ty, tyt, bz, bzt):
    r = pl.program_id(0)

    def band(distance, axis):
        out = jnp.zeros(distance.shape, f32)
        for t in range(TAPS):
            out = jnp.where(distance == t, taps[r, axis * TAPS + t], out)
        return out

    def circulant(row, n):
        wide = jnp.broadcast_to(row[0:1], (n, row.shape[1]))
        return pltpu.roll(wide, 0, 1, stride=1, stride_axis=0).astype(bf16)

    m = iota((8, EXR), 1)
    aligned = lax.bitwise_and(m, ZI - 1) == 0
    taps_at = band(lax.shift_right_logical(m, 3) - 1, 1)
    kx[r] = circulant(jnp.where(aligned, taps_at, 0.0), XR)
    taps_at = band(lax.shift_right_logical(EXR - m, 3) - 1, 1)
    kxt[r] = circulant(jnp.where(aligned, taps_at, 0.0), EXR)[:, :XR]
    n = iota((8, YE), 1)
    apart = jnp.where(n < YE // 2, n, n - YE)
    ty[r] = circulant(band(HALF - apart, 2), YE)
    back = circulant(band(HALF + apart, 2), YE)
    tyt[r] = back

    def parts(x):
        group = jnp.where(x >= 2 * GR, 2, jnp.where(x >= GR, 1, 0))
        within = x - group * GR
        return group * ZI + lax.bitwise_and(within, ZI - 1), lax.shift_right_logical(within, 3)

    (zr, xr), (zc, xc) = parts(iota((ZR, 1), 0)), parts(iota((1, ZR), 1))
    same = xr == xc
    bz[r] = jnp.where(same, band(zc - zr + HALF, 0), 0.0).astype(bf16)
    bzt[r] = jnp.where(same, band(zr - zc + HALF, 0), 0.0).astype(bf16)


MATS = [(XR, EXR), (EXR, XR), (YE, YE), (YE, YE), (ZR, ZR), (ZR, ZR)]


def bands(taps):
    return pl.pallas_call(
        bands_body,
        grid=(VIEWS,),
        out_shape=tuple(pltpu.VMEM((VIEWS,) + s, bf16) for s in MATS),
        in_specs=[pl.BlockSpec(memory_space=pltpu.SMEM)],
        out_specs=(KEPT,) * len(MATS),
        compiler_params=params(),
        cost_estimate=cost(4e9, 2e7),
    )(taps)


def cell_body(place, start, own, left, right, scratch):
    layer = place[1]
    last = start.shape[2] - 128
    after = jnp.minimum((layer + 1) * YQ, last)
    before = jnp.maximum(layer * YQ - 128, 0)
    lane = iota((BX, 128), 1)
    for z in range(NZ):
        rows = pl.ds(z // ZI * XR + z % ZI, BX, stride=ZI)
        for c in range(2):
            at = pl.multiple_of(layer * YQ + c * 128, 128)
            scratch[c, rows, :] = start[z, :, pl.ds(at, 128)]
        head = start[z, :, pl.ds(pl.multiple_of(after, 128), 128)]
        tail = start[z, :, pl.ds(pl.multiple_of(before, 128), 128)]
        head = jnp.where((lane < TURN - YQ) & (layer < VIEWS - 1), head, 0.0)
        tail = jnp.where((lane >= TURN - YQ) & (layer > 0), tail, 0.0)
        scratch[2, rows, :] = head + tail
    value = jnp.concatenate([scratch[c] for c in range(3)], axis=1)
    own[...] = value.reshape(ZG, XR, YE)
    code = to_code(value * E_SCALE).reshape(ZG, XR, YE)
    left[...] = code[:, : XR // 2]
    right[...] = code[:, XR // 2 :]


def cell(place, start):
    half = jax.ShapeDtypeStruct((ZG, XR // 2, YE), i16)
    return pl.pallas_call(
        cell_body,
        out_shape=(pltpu.VMEM((ZG, XR, YE), f32), half, half),
        in_specs=[
            pl.BlockSpec(memory_space=pltpu.SMEM),
            pl.BlockSpec(memory_space=pltpu.VMEM),
        ],
        scratch_shapes=[pltpu.VMEM((3, ROWS, 128), f32)],
        compiler_params=params(),
        cost_estimate=cost(3e6, 6e6),
    )(place, start)


def blurred_columns(field, kx, out):
    for g in range(ZG):
        x = dot(kx[...].reshape(VIEWS * XR, EXR), field[g]).astype(bf16)
        out[:, g * XR : (g + 1) * XR, :] = x.reshape(VIEWS, XR, YE)


def blurred(x, ty, bz):
    y = dot(x, ty).astype(bf16)
    return [dot(bz, columns_of(y, XR, c)) for c in range(BX // GX)]


def columns_of(rows, stride, c):
    return jnp.concatenate(
        [rows[g * stride + c * GR : g * stride + (c + 1) * GR] for g in range(ZG)], axis=0
    )


def rows_from(groups):
    return jnp.concatenate(
        [part[g * GR : (g + 1) * GR] for g in range(ZG) for part in groups], axis=0
    )


def mirrored(quotient, kxt, tyt, bzt, out, first):
    y = dot(quotient, tyt).astype(bf16)
    x = [dot(kxt, y[g * XR : (g + 1) * XR]).astype(bf16) for g in range(ZG)]
    for c in range(EX // GX):
        rows = slice(c * GR, (c + 1) * GR)
        z = dot(bzt, jnp.concatenate([part[rows] for part in x], axis=0))
        for g in range(ZG):
            part = z[g * GR : (g + 1) * GR]
            out[g, rows, :] = part if first else out[g, rows, :] + part


def quotient_of(layer, code, blur_now):
    lane = iota(code.shape, 1)
    inside = (lane < YQ) | ((lane < TURN) & (layer < VIEWS - 1)) | ((lane >= TURN) & (layer > 0))
    measured = jnp.where(inside, from_code(code) * (1.0 / M_SCALE) + M_MID, 0.0)
    return (measured / jnp.where(inside, blur_now, 1.0)).astype(bf16)


def widened(own, from_left, from_right):
    inverse = 1.0 / E_SCALE
    return jnp.concatenate(
        [from_code(from_left) * inverse, own, from_code(from_right) * inverse], axis=1
    )


def blur_body(own, from_left, from_right, kx, ty, bz, out, field, columns):
    step = pl.program_id(0)

    @pl.when(step == 0)
    def _():
        field[...] = widened(own[...], from_left[...], from_right[...]).astype(bf16)
        blurred_columns(field, kx, columns)

    out[step] = rows_from(blurred(columns[step], ty[step], bz[step]))


def blur(own, from_left, from_right, mats):
    operands = kept([own, from_left, from_right, mats[0], mats[2], mats[4]])
    return pl.pallas_call(
        blur_body,
        grid=(VIEWS,),
        out_shape=pltpu.VMEM((VIEWS, ROWS, YE), f32),
        in_specs=[KEPT] * len(operands),
        out_specs=KEPT,
        scratch_shapes=[pltpu.VMEM((ZG, EXR, YE), bf16), pltpu.VMEM((VIEWS, ROWS, YE), bf16)],
        compiler_params=params(),
        cost_estimate=cost(7e9, 1.6e7),
    )(*operands)


def joined(parts):
    return jnp.concatenate([untucked(part) for part in parts], axis=0)


def grouped(refs, layout):
    refs = iter(refs)
    return [[next(refs) for _ in range(n)] for n in layout]


def mirror_body(views, layout, first, last, place, *rest):
    rest = list(rest)
    before = None if first else rest.pop(0)
    codes, rest = grouped(rest, layout), rest[sum(layout) :]
    blur_ref, kxt, tyt, bzt, total = rest[:5]
    if not first:
        total[...] = before[...]
    for r, parts in zip(views, codes):
        quotient = quotient_of(place[1], joined(parts), blur_ref[r])
        mirrored(quotient, kxt[r], tyt[r], bzt[r], total, first)
    if last:
        left, right = flat(total[:, : EXR // 2]), flat(total[:, EXR // 2 :])
        send_sides(send_wide, place, rest[5], rest[6], left, right, rest[7])


def mirror(place, before, codes, views, blur_all, mats, last):
    first = before is None
    layout = tuple(len(parts) for parts in codes)
    columns = jax.ShapeDtypeStruct((wide_rows(ZG * EXR // 2), YQ), i16)
    operands = [] if first else [before]
    operands += [part for parts in codes for part in parts]
    operands = kept(operands + [blur_all, mats[1], mats[3], mats[5]])
    return pl.pallas_call(
        functools.partial(mirror_body, views, layout, first, last),
        out_shape=(pltpu.VMEM((ZG, EXR, YE), f32),) + (columns,) * (2 * last),
        in_specs=[pl.BlockSpec(memory_space=pltpu.SMEM)] + [KEPT] * len(operands),
        out_specs=(KEPT,) * (1 + 2 * last),
        scratch_shapes=[pltpu.VMEM((2,) + columns.shape, i16)] * last,
        compiler_params=params(),
        cost_estimate=cost(2e9 * len(views), 8e6 * len(views)),
    )(place, *operands)


def second_body(layout, place, own, e_left, e_right, total, x_first, x_second, *rest):
    codes, rest = grouped(rest, layout), rest[sum(layout) :]
    kx, kxt, ty, tyt, bz, bzt = rest[:6]
    estimate, center, first, second, field, columns, acc, sides, held, sent = rest[6:]
    take_sides(place, x_first, x_second, sides)
    edge = MARGIN * ZI
    middle = EXR // 2
    start = widened(own[...], e_left[...], e_right[...]) * (1.0 / VIEWS)
    for half in range(2):
        came = sides.at[half]
        rows = slice(half * middle, (half + 1) * middle)
        now = start[:, rows] * (total[:, rows] + wide_value(came).reshape(ZG, middle, YE))
        field[:, rows] = now.astype(bf16)
        inner = now[:, edge:] if half == 0 else now[:, : middle - edge]
        estimate[:, half * edge : (half + 1) * edge] = inner[:, :, :YQ]
    blurred_columns(field, kx, columns)
    for r in range(VIEWS):
        held[r] = joined(codes[r])
    acc[...] = jnp.zeros_like(acc)

    def two_views(i, _):
        for r in (2 * i, 2 * i + 1):
            blur_now = rows_from(blurred(columns[r], ty[r], bz[r]))
            quotient = quotient_of(place[1], held[r], blur_now)
            mirrored(quotient, kxt[r], tyt[r, :, :YQ], bzt[r], acc, False)
        return 0

    lax.fori_loop(0, VIEWS // 2, two_views, 0)
    center[...] = acc[:, edge : edge + XR, :]
    left, right = flat(acc[:, :edge, :]), flat(acc[:, edge + XR :, :])
    send_sides(send, place, first, second, left, right, sent)


def second(place, own, e_left, e_right, total, x_first, x_second, codes, mats):
    columns = jax.ShapeDtypeStruct((ZG * MARGIN * ZI + 16, YQ), i16)
    cell_shape = pltpu.VMEM((ZG, XR, YQ), f32)
    layout = tuple(len(parts) for parts in codes)
    operands = [own, e_left, e_right, total, x_first, x_second]
    operands += [part for parts in codes for part in parts] + list(mats)
    operands = kept(operands)
    return pl.pallas_call(
        functools.partial(second_body, layout),
        out_shape=(cell_shape, cell_shape, columns, columns),
        in_specs=[pl.BlockSpec(memory_space=pltpu.SMEM)] + [KEPT] * len(operands),
        out_specs=(KEPT,) * 4,
        scratch_shapes=[
            pltpu.VMEM((ZG, EXR, YE), bf16),
            pltpu.VMEM((VIEWS, ROWS, YE), bf16),
            pltpu.VMEM((ZG, EXR, YQ), f32),
            pltpu.VMEM((2,) + x_first.shape, i16),
            pltpu.VMEM((VIEWS, ROWS, YE), i16),
            pltpu.VMEM((2,) + columns.shape, i16),
        ],
        compiler_params=params(),
        cost_estimate=cost(1.6e10, 4e7),
    )(place, *operands)


def finish_body(place, estimate, total, x_first, x_second, low, high, sides):
    take_sides(place, x_first, x_second, sides)
    middle = XR // 2
    a = total[:, :middle] + lane_value(sides.at[0]).reshape(ZG, middle, YQ)
    b = total[:, middle:] + lane_value(sides.at[1]).reshape(ZG, middle, YQ)
    send(low, flat(estimate[:, :middle] * a * (1.0 / VIEWS)))
    send(high, flat(estimate[:, middle:] * b * (1.0 / VIEWS)))


def finish(place, estimate, total, x_first, x_second):
    half = jax.ShapeDtypeStruct((ROWS // 2 + 16, YQ), i16)
    return pl.pallas_call(
        finish_body,
        out_shape=(half, half),
        in_specs=[pl.BlockSpec(memory_space=pltpu.SMEM)] + [KEPT] * 4,
        out_specs=(KEPT, KEPT),
        scratch_shapes=[pltpu.VMEM((2,) + x_first.shape, i16)],
        compiler_params=params(),
        cost_estimate=cost(5e6, 4e6),
    )(place, *kept([estimate, total, x_first, x_second]))


def spread_out(codes, scratch, store):
    middle = XR // 2
    for half in range(2):
        value = lane_value(codes[half])
        for c in range(2):
            scratch[half, c] = value[:, c * 128 : (c + 1) * 128]
            for z in range(NZ):
                rows = pl.ds(z // ZI * middle + z % ZI, BX // 2, stride=ZI)
                store(z, half, c, scratch[half, c, rows, :])


def gather_body(place, *rest):
    codes, out, scratch = rest[: 2 * VIEWS - 2], rest[2 * VIEWS - 2], rest[2 * VIEWS - 1]
    for i, r in enumerate((0, 1, 3)):
        at = lax.rem(place[1] + VIEWS - r, VIEWS) * YQ

        def store(z, half, c, value):
            lanes = pl.ds(pl.multiple_of(at + c * 128, 128), 128)
            out[z, half * BX // 2 : (half + 1) * BX // 2, lanes] = value

        spread_out(codes[2 * i : 2 * i + 2], scratch.at[i], store)


def gathered(place, codes):
    return pl.pallas_call(
        gather_body,
        out_shape=jax.ShapeDtypeStruct((NZ, BX, VIEWS * YQ), f32),
        in_specs=[pl.BlockSpec(memory_space=pltpu.SMEM)] + [KEPT] * len(codes),
        scratch_shapes=[pltpu.VMEM((VIEWS - 1, 2, 2, ROWS // 2, 128), f32)],
        compiler_params=params(),
        cost_estimate=cost(3e6, 6e6),
    )(place, *kept(codes))


def complete_body(place, low, high, _, out, scratch, quarter, sem):
    def store(z, half, c, value):
        quarter[z, half * BX // 2 : (half + 1) * BX // 2, c * 128 : (c + 1) * 128] = value

    spread_out((low, high), scratch, store)
    at = pl.multiple_of(lax.rem(place[1] + 2, VIEWS) * YQ, YQ)
    move = pltpu.make_async_copy(quarter, out.at[:, :, pl.ds(at, YQ)], sem)
    move.start()
    move.wait()


def completed(place, low, high, out):
    anywhere = pl.BlockSpec(memory_space=pl.ANY)
    vmem = pl.BlockSpec(memory_space=pltpu.VMEM)
    return pl.pallas_call(
        complete_body,
        out_shape=jax.ShapeDtypeStruct(out.shape, f32),
        in_specs=[pl.BlockSpec(memory_space=pltpu.SMEM), vmem, vmem, anywhere],
        out_specs=anywhere,
        input_output_aliases={3: 0},
        scratch_shapes=[
            pltpu.VMEM((2, 2, ROWS // 2, 128), f32),
            pltpu.VMEM((NZ, BX, YQ), f32),
            pltpu.SemaphoreType.DMA,
        ],
        compiler_params=params(),
        cost_estimate=cost(1e6, 2e6),
    )(place, *kept([low, high]), out)


def per_device(view_tiles, route_block, route_column, psf_taps, start_estimate):
    groups = lax.axis_size("block")
    cap = max(2, (2 * BX + groups - 1) // groups)
    me, layer = lax.axis_index("block"), lax.axis_index("view")
    place = jnp.stack([me, layer]).astype(i32)

    def around(x, shift):
        return lax.ppermute(x, "view", [(i, (i + shift) % VIEWS) for i in range(VIEWS)])

    def shifted(x, shift):
        pairs = [(i, i + shift) for i in range(groups) if 0 <= i + shift < groups]
        return lax.ppermute(x, "block", pairs)

    def swapped(x, start):
        pairs = []
        for i in range(start, groups - 1, 2):
            pairs += [(i, i + 1), (i + 1, i)]
        return lax.ppermute(x, "block", pairs) if pairs else jnp.zeros_like(x)

    outgoing = pack(cap, groups, route_block[0], route_column[0], view_tiles[0])
    arrived = lax.all_to_all(outgoing, "block", split_axis=0, concat_axis=0, tiled=True)

    psf, start_estimate, _ = lax.optimization_barrier((psf_taps[0], start_estimate, outgoing))
    kernel = psf / jnp.sum(psf, axis=1, keepdims=True)
    kernel = kernel.astype(bf16).astype(f32)
    taps = [kernel] + [around(kernel, r) for r in range(1, VIEWS)]
    own, to_left, to_right = cell(place, start_estimate)
    e_left, e_right = shifted(to_right, 1), shifted(to_left, -1)

    codes = unpack(cap, place, arrived)
    own, taps, codes = lax.optimization_barrier((own, taps, codes))
    low_on, high_on = around(codes[2], 1), around(codes[3], -1)
    codes = [
        [codes[0]],
        [around(codes[1], 1)],
        [around(low_on, 1), around(high_on, -1)],
        [around(codes[4], -1)],
    ]
    mats = bands(jnp.stack(taps).reshape(VIEWS, 3 * TAPS))
    blur_all = blur(own, e_left, e_right, mats)
    (total,) = mirror(place, None, codes[:1], [0], blur_all, mats, False)
    (total,) = mirror(place, total, [codes[1], codes[3]], [1, 3], blur_all, mats, False)
    total, first, second_part = mirror(place, total, codes[2:3], [2], blur_all, mats, True)
    x_first, x_second = swapped(first, 1), swapped(second_part, 0)
    estimate, center, first, second_part = second(
        place, own, e_left, e_right, total, x_first, x_second, codes, mats
    )
    x_first, x_second = swapped(first, 1), swapped(second_part, 0)
    low, high = finish(place, estimate, center, x_first, x_second)
    low_after, high_before = around(low, -1), around(high, 1)
    high_after, low_before = around(high, -1), around(low, 1)
    low_across, high_across = around(low_after, -1), around(high_before, 1)
    out = gathered(place, [low, high, low_before, high_before, low_after, high_after])
    return completed(place, low_across, high_across, out)


def solution(mesh):
    placed = (
        P("view", "block", None, None),
        P("view", "block"),
        P("view", "block"),
        P("view", None, None),
        P(None, "block", None),
    )
    return jax.shard_map(
        per_device, mesh=mesh, in_specs=placed, out_specs=P(None, "block", None), check_vma=False
    )
```
